32 devices in a mesh: seq: 4 (over z), tensor: 8 (over y, x, core).
Axes of the slice: x: 2, y: 2, z: 4, core: 2. Of those that a mesh axis runs over, the one named last changes fastest.
Arguments:
- hidden: bfloat16 [4, 128, 8192], P('seq', None, 'tensor'), may hold values from -2.5 to 2.5
- neighbours: bfloat16 [4, 8, 128, 1024], P('seq', 'tensor'), may hold values from -2.5 to 2.5
- slot_of: int32 [4, 2, 2], P('seq'), may hold values from 0 to 7, as said below
- w_query: bfloat16 [8192, 8192], P(None, 'tensor'), may hold values from -0.0625 to 0.0625
- w_key: bfloat16 [1024, 8192], P(None, 'tensor'), may hold values from -0.1875 to 0.1875
- w_value: bfloat16 [1024, 8192], P(None, 'tensor'), may hold values from -0.1875 to 0.1875
- out_grad: bfloat16 [4, 128, 8192], P('seq', None, 'tensor'), may hold values from -4 to 4
Outputs:
- attended: bfloat16 [4, 128, 8192], P('seq', None, 'tensor')
- hidden_grad: bfloat16 [4, 128, 8192], P('seq', None, 'tensor')
- neighbour_grad: bfloat16 [4, 8, 128, 1024], P('seq', 'tensor')
- query_weight_grad: float32 [8192, 8192], P('seq', 'tensor')
- key_weight_grad: float32 [1024, 8192], P('seq', 'tensor')
- value_weight_grad: float32 [1024, 8192], P('seq', 'tensor')
The draws below stay inside these ranges and needn't reach their ends.
Inputs may be any that keep to these rules, and one draw needn't show every extreme that they name: `slot_of`: slot j of a sequence's group is slot j % 1 of tensor device j; the 4 entries of one sequence are distinct.
All inputs are finite; a program needn't handle non-finite values.
Results may differ from the reference program's by a relative error of at most 0.013.
Values may be sent and summed in bfloat16 or wider, within the bound.
A program may use at most 192 MiB of HBM per device.

```python
import math
import jax
import jax.numpy as jnp
from jax import lax

D = 8192
HEADS = 64
HS = 128
DE = 1024
SPAN = 64
NB = 2
R = 128
SEQS = 4
SPANS = 2
LEN = 128
NEIGH = 4
SLOT_ALL = 8
N_TENSOR = 8


def draw_slot_of(key, part):
    key = jax.random.fold_in(key, 7)
    seq_keys = jax.random.split(key, SEQS)

    def one_sequence(seq_key):
        first_key, second_key = jax.random.split(seq_key)
        inner = jax.random.permutation(first_key, SLOT_ALL - 2) + 1
        ends = jnp.array([0, SLOT_ALL - 1], jnp.int32)
        chosen = jnp.concatenate([ends, inner[:NEIGH - 2].astype(jnp.int32)])
        order = jax.random.permutation(second_key, NEIGH)
        return chosen[order].reshape(SPANS, NB)
    return jax.vmap(one_sequence)(seq_keys).astype(jnp.int32)


def steps_of(rng, dims, shards, low, largest):
    loudness, own = 1.0, jax.random.fold_in(rng, 6)
    for dim, shards_of in shards:
        draws = jnp.exp(jax.random.uniform(jax.random.fold_in(own, dim), (shards_of,), jnp.float32, low / len(shards), largest / len(shards)))
        loudness = loudness * jnp.repeat(draws, dims[dim] // shards_of).reshape([-1 if axis == dim else 1 for axis in range(len(dims))])
    return loudness


def noise(key, dims, scale, most, pieces=(), dtype=jnp.bfloat16):
    values = jax.random.normal(key, dims, jnp.float32) * scale
    if len(pieces) > 0:
        values = steps_of(key, dims, pieces, -0.22, 0.18) * values
    return jnp.clip(values, min=-most, max=most).astype(dtype)


def setup_inputs(seed: int = 0) -> dict:
    key_list = jax.random.split(jax.random.key(seed), 8)
    hidden = noise(key_list[0], (SEQS, LEN, D), 1.0, 2.5, ((0, 4), (2, 8)))
    neighbours = noise(key_list[1], (SEQS, SLOT_ALL, R, DE), 1.0, 2.5, ((0, 4), (1, 8)))
    slot_of = draw_slot_of(jax.random.fold_in(key_list[7], 71), 0)
    w_query = noise(key_list[3], (D, HEADS * HS), D ** -0.5, 0.0625, ((1, 8),))
    w_key = noise(key_list[4], (DE, HEADS * HS), DE ** -0.5, 0.1875, ((1, 8),))
    w_value = noise(key_list[5], (DE, HEADS * HS), DE ** -0.5, 0.1875, ((1, 8),))
    out_grad = noise(key_list[6], (SEQS, LEN, HEADS * HS), 1.0, 4.0, ((0, 4), (2, 8)))
    return dict(hidden=hidden, neighbours=neighbours, slot_of=slot_of, w_query=w_query, w_key=w_key, w_value=w_value, out_grad=out_grad)


def contract_rows(left, right):
    return lax.dot_general(left, right, (((0,), (0,)), ((), ())), preferred_element_type=jnp.float32)

def rounded_sum(total, term):
    return total + lax.optimization_barrier(term.astype(jnp.bfloat16)).astype(jnp.float32)

def reference(hidden, neighbours, slot_of, w_query, w_key, w_value, out_grad):
    width = HEADS * HS
    group = width // N_TENSOR
    lag = SPAN - 1
    scale = 1.0 / math.sqrt(HS)
    attended_all = []
    hidden_all = []
    neighbour_all = []
    query_weight = jnp.zeros((D, width), jnp.float32)
    key_weight = jnp.zeros((DE, width), jnp.float32)
    value_weight = jnp.zeros((DE, width), jnp.float32)
    for sequence in range(SEQS):
        tokens = hidden[sequence]
        query = jnp.dot(tokens, w_query, preferred_element_type=jnp.float32).astype(jnp.bfloat16)
        slots = slot_of[sequence].reshape(-1).astype(jnp.int32)
        picked = neighbours[sequence][slots]
        states = picked.reshape(NEIGH * R, DE)
        keys = jnp.dot(states, w_key, preferred_element_type=jnp.float32).astype(jnp.bfloat16)
        values = jnp.dot(states, w_value, preferred_element_type=jnp.float32).astype(jnp.bfloat16)
        shaped_keys = keys.reshape(SPANS, NB * R, HEADS, HS).astype(jnp.float32)
        shaped_values = values.reshape(SPANS, NB * R, HEADS, HS).astype(jnp.float32)
        blank = jnp.zeros((lag, width), jnp.bfloat16)
        shifted = jnp.concatenate([query[lag:], blank], 0).reshape(SPANS, SPAN, HEADS, HS).astype(jnp.float32)
        grads = jnp.concatenate([out_grad[sequence][lag:], blank], 0).reshape(SPANS, SPAN, HEADS, HS).astype(jnp.float32)
        scores = jnp.einsum('uqhd,ukhd->uhqk', shifted, shaped_keys) * scale
        raised = jnp.exp(scores)
        shares = raised / lax.optimization_barrier(jnp.sum(raised, axis=-1, keepdims=True))
        share_bf = shares.astype(jnp.bfloat16)
        mixed = jnp.einsum('uhqk,ukhd->uqhd', share_bf.astype(jnp.float32), shaped_values).astype(jnp.bfloat16)
        attended_all.append(jnp.concatenate([blank, mixed.reshape(LEN, width)[:LEN - lag]], 0))
        share_grad = jnp.einsum('uqhd,ukhd->uhqk', grads, shaped_values)
        centre = lax.optimization_barrier(jnp.sum(shares * share_grad, axis=-1, keepdims=True))
        score_grad = (shares * (share_grad - centre) * scale).astype(jnp.bfloat16).astype(jnp.float32)
        shift_grad = jnp.einsum('uhqk,ukhd->uqhd', score_grad, shaped_keys).astype(jnp.bfloat16)
        key_grad = jnp.einsum('uhqk,uqhd->ukhd', score_grad, shifted).astype(jnp.bfloat16).reshape(NEIGH * R, width)
        value_grad = jnp.einsum('uhqk,uqhd->ukhd', share_bf.astype(jnp.float32), grads).astype(jnp.bfloat16).reshape(NEIGH * R, width)
        query_grad = jnp.concatenate([blank, shift_grad.reshape(LEN, width)[:LEN - lag]], 0)
        hidden_total = jnp.zeros((LEN, D), jnp.float32)
        neighbour_total = jnp.zeros((NEIGH * R, DE), jnp.float32)
        for part in range(N_TENSOR):
            first = part * group
            last = first + group
            term = jnp.dot(query_grad[:, first:last], w_query[:, first:last].T, preferred_element_type=jnp.float32)
            hidden_total = rounded_sum(hidden_total, term)
            back = jnp.dot(key_grad[:, first:last], w_key[:, first:last].T, preferred_element_type=jnp.float32)
            back = back + jnp.dot(value_grad[:, first:last], w_value[:, first:last].T, preferred_element_type=jnp.float32)
            neighbour_total = rounded_sum(neighbour_total, back)
        hidden_all.append(hidden_total.astype(jnp.bfloat16))
        blocks = neighbour_total.astype(jnp.bfloat16).reshape(NEIGH, R, DE)
        neighbour_all.append(jnp.zeros((SLOT_ALL, R, DE), jnp.bfloat16).at[slots].set(blocks))
        query_weight = query_weight + contract_rows(tokens, query_grad)
        key_weight = key_weight + contract_rows(states, key_grad)
        value_weight = value_weight + contract_rows(states, value_grad)
    return (jnp.stack(attended_all), jnp.stack(hidden_all), jnp.stack(neighbour_all), query_weight, key_weight, value_weight)
```

```python
import math

import jax
import jax.numpy as jnp
from jax import lax
from jax.sharding import PartitionSpec as P

HS = 128
DE = 1024
SPAN = 64
R = 128


def contract_rows(left, right):
    return lax.dot_general(
        left, right, (((0,), (0,)), ((), ())), preferred_element_type=jnp.float32
    )


def contract_cols(left, right):
    return lax.dot_general(
        left, right, (((1,), (1,)), ((), ())), preferred_element_type=jnp.float32
    )


def body(hidden, neighbours, slot_of, w_query, w_key, w_value, out_grad):
    width = w_query.shape[1]
    heads_here = width // HS
    slot_count = neighbours.shape[1]
    span_count = slot_of.shape[1]
    lag = SPAN - 1
    scale = 1.0 / math.sqrt(HS)
    length = hidden.shape[1]
    first = lag // 16 * 16
    skip = lag - first
    whole = lax.all_gather(hidden[0, first:], "tensor", axis=1, tiled=True)
    query = jnp.dot(whole, w_query, preferred_element_type=jnp.float32).astype(jnp.bfloat16)
    slots = slot_of[0].reshape(-1)
    every = lax.all_gather(neighbours, "tensor", axis=1, tiled=True)[0]
    picked = jnp.take(every, slots, axis=0)
    states = picked.reshape(-1, DE)
    keys = jnp.dot(states, w_key, preferred_element_type=jnp.float32).astype(jnp.bfloat16)
    values = jnp.dot(states, w_value, preferred_element_type=jnp.float32).astype(jnp.bfloat16)
    shaped_keys = keys.reshape(span_count, -1, heads_here, HS)
    shaped_values = values.reshape(span_count, -1, heads_here, HS)
    blank = jnp.zeros((lag, width), jnp.bfloat16)
    shifted = jnp.concatenate([query[skip:], blank], 0).reshape(span_count, SPAN, heads_here, HS)
    grads = jnp.concatenate([out_grad[0][lag:], blank], 0).reshape(span_count, SPAN, heads_here, HS)
    scores = (
        jnp.einsum("uqhd,ukhd->uhqk", shifted, shaped_keys, preferred_element_type=jnp.float32)
        * scale
    )
    raised = jnp.exp(scores)
    shares = raised / jnp.sum(raised, axis=-1, keepdims=True)
    share_bf = shares.astype(jnp.bfloat16)
    mixed = jnp.einsum(
        "uhqk,ukhd->uqhd", share_bf, shaped_values, preferred_element_type=jnp.float32
    ).astype(jnp.bfloat16)
    attended = jnp.concatenate([blank, mixed.reshape(length, width)[: length - lag]], 0)[None]
    share_grad = jnp.einsum(
        "uqhd,ukhd->uhqk", grads, shaped_values, preferred_element_type=jnp.float32
    )
    centre = jnp.sum(shares * share_grad, axis=-1, keepdims=True)
    score_grad = (shares * (share_grad - centre) * scale).astype(jnp.bfloat16)
    shift_grad = jnp.einsum(
        "uhqk,ukhd->uqhd", score_grad, shaped_keys, preferred_element_type=jnp.float32
    ).astype(jnp.bfloat16)
    key_grad = (
        jnp.einsum("uhqk,uqhd->ukhd", score_grad, shifted, preferred_element_type=jnp.float32)
        .astype(jnp.bfloat16)
        .reshape(-1, width)
    )
    value_grad = (
        jnp.einsum("uhqk,uqhd->ukhd", share_bf, grads, preferred_element_type=jnp.float32)
        .astype(jnp.bfloat16)
        .reshape(-1, width)
    )
    query_grad = jnp.concatenate(
        [blank[:skip], shift_grad.reshape(length, width)[: length - lag]], 0
    )
    feature_grad = lax.psum_scatter(
        contract_cols(query_grad, w_query).astype(jnp.bfloat16),
        "tensor",
        scatter_dimension=1,
        tiled=True,
    )
    early = jnp.zeros((first, feature_grad.shape[1]), jnp.bfloat16)
    hidden_grad = jnp.concatenate([early, feature_grad], 0)[None]
    local_term = contract_cols(key_grad, w_key) + contract_cols(value_grad, w_value)
    flat_bf = local_term.astype(jnp.bfloat16).reshape(slots.shape[0], -1)
    wanted = lax.iota(jnp.int32, slot_count * lax.axis_size("tensor"))
    select = (wanted[:, None] == slots[None, :]).astype(jnp.bfloat16)
    placed = lax.psum_scatter(
        jnp.dot(select, flat_bf, preferred_element_type=jnp.float32).astype(jnp.bfloat16),
        "tensor",
        scatter_dimension=0,
        tiled=True,
    )
    neighbour_grad = placed.reshape(1, slot_count, R, DE)
    tokens_all = lax.all_to_all(whole, "seq", split_axis=1, concat_axis=0, tiled=True)
    grads_all = lax.all_gather(query_grad, "seq", axis=0, tiled=True)
    query_part = contract_rows(tokens_all, grads_all)
    both = contract_rows(states, jnp.concatenate([key_grad, value_grad], 1))
    both = lax.psum_scatter(
        both.astype(jnp.bfloat16), "seq", scatter_dimension=0, tiled=True
    ).astype(jnp.float32)
    return (attended, hidden_grad, neighbour_grad, query_part, both[:, :width], both[:, width:])


def solution(mesh):
    return jax.shard_map(
        body,
        mesh=mesh,
        in_specs=(
            P("seq", None, "tensor"),
            P("seq", "tensor", None, None),
            P("seq", None, None),
            P(None, "tensor"),
            P(None, "tensor"),
            P(None, "tensor"),
            P("seq", None, "tensor"),
        ),
        out_specs=(
            P("seq", None, "tensor"),
            P("seq", None, "tensor"),
            P("seq", "tensor", None, None),
            P("seq", "tensor"),
            P("seq", "tensor"),
            P("seq", "tensor"),
        ),
        check_vma=False,
    )
```

```python
import functools
import math

import jax
import jax.numpy as jnp
from jax import lax
from jax.experimental import pallas as pl
from jax.experimental.pallas import tpu as pltpu
from jax.sharding import PartitionSpec as P

HS = 128
DE = 1024
SPAN = 64
R = 128
TAIL = 16
MESH = pl.DeviceIdType.MESH
BF = jnp.bfloat16
F32 = jnp.float32
VMEM = pl.BlockSpec(memory_space=pltpu.VMEM)
ANY = pl.BlockSpec(memory_space=pl.ANY)
LIMIT = 50 * 2**20


def contract_rows(left, right):
    return lax.dot_general(left, right, (((0,), (0,)), ((), ())), preferred_element_type=F32)


def contract_cols(left, right):
    return lax.dot_general(left, right, (((1,), (1,)), ((), ())), preferred_element_type=F32)


def remote(src, dst, send, recv, axis, index):
    return pltpu.make_async_remote_copy(
        src_ref=src, dst_ref=dst, send_sem=send, recv_sem=recv,
        device_id={axis: index}, device_id_type=MESH,
    )


def gather_kernel(
    n, seqs, hid, nb, og, w_hbm, whole, every, qall, ogall,
    w, acc, w_sem, h_send, h_recv, n_send, n_recv, z_send, z_recv,
):
    me = lax.axis_index("tensor")
    row = lax.axis_index("seq")
    chips = n // 2
    core = lax.rem(me, 2)
    chip = me // 2
    twin = me + 1 - 2 * core
    depth = hid.shape[1]

    def peer(k):
        return lax.rem(chip + k, chips) * 2 + core

    def over(k):
        return lax.rem(row + k, seqs)

    fetch = pltpu.make_async_copy(w_hbm, w, w_sem)
    fetch.start()
    barrier = pltpu.get_barrier_semaphore()
    pl.semaphore_signal(barrier, inc=1, device_id={"tensor": twin}, device_id_type=MESH)

    @pl.loop(1, chips)
    def _(k):
        pl.semaphore_signal(barrier, inc=1, device_id={"tensor": peer(k)}, device_id_type=MESH)

    for k in range(1, seqs):
        pl.semaphore_signal(barrier, inc=1, device_id={"seq": over(k)}, device_id_type=MESH)
    pl.semaphore_wait(barrier, chips + seqs - 1)

    def own(ref, out, send, recv, k, target):
        return remote(ref, out.at[me], send.at[k], recv.at[me], "tensor", target)

    def onward(out, send, recv, k):
        return remote(
            out.at[peer(k)], out.at[peer(k)], send.at[chips + k], recv.at[peer(k)], "tensor", twin
        )

    def arrival(out, send, recv, index):
        return remote(out.at[index], out.at[index], send.at[0], recv.at[index], "tensor", twin)

    def z_copy(ref, out, lane, k):
        return remote(ref, out.at[row], z_send.at[lane, k], z_recv.at[lane, row], "seq", over(k))

    @pl.loop(1, chips)
    def _(k):
        own(hid, whole, h_send, h_recv, k, peer(k)).start()

    own(hid, whole, h_send, h_recv, 0, twin).start()

    @pl.loop(1, chips)
    def _(k):
        own(nb, every, n_send, n_recv, k, peer(k)).start()

    own(nb, every, n_send, n_recv, 0, twin).start()
    for k in range(1, seqs):
        z_copy(og, ogall, 0, k).start()
    whole[me] = hid[...]
    every[me] = nb[...]
    ogall[row] = og[...]
    fetch.wait()

    def add(index):
        part = w[pl.ds(pl.multiple_of(index * depth, depth), depth), :]
        acc[...] += jnp.dot(whole[index], part, preferred_element_type=F32)

    acc[...] = jnp.zeros_like(acc)
    add(me)

    @pl.loop(1, chips)
    def _(k):
        arrival(whole, h_send, h_recv, peer(k)).wait_recv()
        onward(whole, h_send, h_recv, k).start()
        add(peer(k))

    @pl.loop(0, chips)
    def _(k):
        index = peer(k) + 1 - 2 * core
        arrival(whole, h_send, h_recv, index).wait_recv()
        add(index)

    qall[row] = acc[...].astype(BF)
    for k in range(1, seqs):
        z_copy(qall.at[row], qall, 1, k).start()

    @pl.loop(1, chips)
    def _(k):
        arrival(every, n_send, n_recv, peer(k)).wait_recv()
        onward(every, n_send, n_recv, k).start()

    @pl.loop(0, chips)
    def _(k):
        arrival(every, n_send, n_recv, peer(k) + 1 - 2 * core).wait_recv()

    for k in range(1, seqs):
        came = over(k)
        for lane, out in ((0, ogall), (1, qall)):
            remote(
                out.at[came], out.at[came], z_send.at[lane, 0], z_recv.at[lane, came], "seq", came
            ).wait_recv()
            z_copy(og if lane == 0 else qall.at[row], out, lane, k).wait_send()
    for ref, out, send, recv in ((hid, whole, h_send, h_recv), (nb, every, n_send, n_recv)):
        own(ref, out, send, recv, 0, twin).wait_send()

        @pl.loop(1, chips)
        def _(k):
            own(ref, out, send, recv, k, peer(k)).wait_send()
            onward(out, send, recv, k).wait_send()


def gather(n, seqs, hid, nb, og, w_query):
    rows, depth = hid.shape
    width = w_query.shape[1]
    dma = pltpu.SemaphoreType.DMA
    return pl.pallas_call(
        functools.partial(gather_kernel, n, seqs),
        out_shape=(
            jax.ShapeDtypeStruct((n, rows, depth), BF),
            jax.ShapeDtypeStruct((n,) + nb.shape, BF),
            jax.ShapeDtypeStruct((seqs, rows, width), BF),
            jax.ShapeDtypeStruct((seqs, rows, width), BF),
        ),
        in_specs=[VMEM, VMEM, VMEM, ANY],
        out_specs=(VMEM,) * 4,
        scratch_shapes=[
            pltpu.VMEM(w_query.shape, BF),
            pltpu.VMEM((rows, width), F32),
            dma, dma((n,)), dma((n,)), dma((n,)), dma((n,)), dma((2, seqs)), dma((2, seqs)),
        ],
        compiler_params=pltpu.CompilerParams(
            collective_id=0, has_side_effects=True, vmem_limit_bytes=LIMIT
        ),
        name="gather",
    )(hid, nb, og, w_query)


def attention_kernel(spans, q, og, key, value, mixed, qg, kg, vg, sgsh):
    scale = 1.0 / math.sqrt(HS)
    reach = key.shape[0] // spans
    for u in range(spans):
        here = pl.ds(u * SPAN, SPAN if u < spans - 1 else TAIL)
        rows = pl.ds(u * reach, reach)
        qu, gu, ku, vu = q[here, :], og[here, :], key[rows, :], value[rows, :]
        raised = jnp.exp(contract_cols(qu, ku) * scale)
        shares = raised / jnp.sum(raised, axis=-1, keepdims=True)
        share_bf = shares.astype(BF)
        mixed[here, :] = jnp.dot(share_bf, vu, preferred_element_type=F32).astype(BF)
        share_grad = contract_cols(gu, vu)
        centre = jnp.sum(shares * share_grad, axis=-1, keepdims=True)
        score_grad = (shares * (share_grad - centre) * scale).astype(BF)
        qg[here, :] = jnp.dot(score_grad, ku, preferred_element_type=F32).astype(BF)
        kg[rows, :] = contract_rows(score_grad, qu).astype(BF)
        vg[rows, :] = contract_rows(share_bf, gu).astype(BF)
        sgsh[0, 0, here, :] = score_grad
        sgsh[1, 0, here, :] = share_bf


def attention(spans, q, og, keys, values):
    rows, width = q.shape
    heads = width // HS
    many = keys.shape[0]
    narrow = pl.BlockSpec((rows, HS), lambda h: (0, h))
    tall = pl.BlockSpec((many, HS), lambda h: (0, h))
    reach = many // spans
    return pl.pallas_call(
        functools.partial(attention_kernel, spans),
        grid=(heads,),
        out_shape=(
            jax.ShapeDtypeStruct((rows, width), BF),
            jax.ShapeDtypeStruct((rows, width), BF),
            jax.ShapeDtypeStruct((many, width), BF),
            jax.ShapeDtypeStruct((many, width), BF),
            jax.ShapeDtypeStruct((2, heads, rows, reach), BF),
        ),
        in_specs=[narrow, narrow, tall, tall],
        out_specs=(
            narrow, narrow, tall, tall,
            pl.BlockSpec((2, 1, rows, reach), lambda h: (0, h, 0, 0)),
        ),
        compiler_params=pltpu.CompilerParams(vmem_limit_bytes=LIMIT),
        name="attention",
    )(q, og, keys, values)


def exchange_kernel(
    n, seqs, hs, ns, sgsh, qg, hid, nbr, zall, qgall,
    h_in, n_in, h_send, h_recv, n_send, n_recv, z_send, z_recv,
):
    me = lax.axis_index("tensor")
    row = lax.axis_index("seq")

    def peer(k):
        return lax.rem(me + k, n)

    barrier = pltpu.get_barrier_semaphore()

    @pl.loop(1, n)
    def _(k):
        pl.semaphore_signal(barrier, inc=1, device_id={"tensor": peer(k)}, device_id_type=MESH)

    for k in range(1, seqs):
        pl.semaphore_signal(
            barrier, inc=1, device_id={"seq": lax.rem(row + k, seqs)}, device_id_type=MESH
        )
    pl.semaphore_wait(barrier, n - 1 + seqs - 1)

    def scatter(ref, into, send, recv, k):
        return remote(ref.at[peer(k)], into.at[me], send.at[k], recv.at[me], "tensor", peer(k))

    outs = (qgall, zall)
    owns = (qg, sgsh)

    def hop(side, h, lane):
        step = 1 - 2 * side
        origin = row - step * h
        src = owns[lane] if h == 0 else outs[lane].at[origin]
        return remote(
            src, outs[lane].at[origin], z_send.at[side, h, lane], z_recv.at[side, h, lane],
            "seq", row + step,
        )

    def sends(side, h):
        if side == 0:
            return (row - h >= 0) & (row + 1 < seqs)
        return (row + h < seqs) & (row >= 1)

    def arrives(side, h):
        return row - 1 - h >= 0 if side == 0 else row + 1 + h < seqs

    def arrived(side, h, lane):
        step = 1 - 2 * side
        origin = row - step * (h + 1)
        return remote(
            outs[lane].at[origin], outs[lane].at[origin],
            z_send.at[side, h, lane], z_recv.at[side, h, lane], "seq", row - step,
        )

    for side in range(2):
        @pl.when(sends(side, 0))
        def _():
            for lane in range(2):
                hop(side, 0, lane).start()

    @pl.loop(1, n)
    def _(k):
        scatter(hs, h_in, h_send, h_recv, k).start()
        scatter(ns, n_in, n_send, n_recv, k).start()

    for lane in range(2):
        outs[lane][row] = owns[lane][...]
    for h in range(seqs - 1):
        for lane in range(2):
            for side in range(2):
                @pl.when(arrives(side, h))
                def _():
                    arrived(side, h, lane).wait_recv()

                if h + 1 < seqs - 1:
                    @pl.when(sends(side, h + 1))
                    def _():
                        hop(side, h + 1, lane).start()

        if h == 0:
            for ref, into, send, recv, out in (
                (hs, h_in, h_send, h_recv, hid), (ns, n_in, n_send, n_recv, nbr)
            ):
                @pl.loop(1, n)
                def _(k):
                    remote(
                        into.at[peer(k)], into.at[peer(k)], send.at[0], recv.at[peer(k)],
                        "tensor", peer(k),
                    ).wait_recv()

                into[me] = ref[me]
                total = into[0].astype(F32)
                for j in range(1, n):
                    total = total + into[j].astype(F32)
                out[...] = total.astype(BF)

    for side in range(2):
        for h in range(seqs - 1):
            @pl.when(sends(side, h))
            def _():
                for lane in range(2):
                    hop(side, h, lane).wait_send()

    @pl.loop(1, n)
    def _(k):
        scatter(hs, h_in, h_send, h_recv, k).wait_send()
        scatter(ns, n_in, n_send, n_recv, k).wait_send()


def exchange(n, seqs, hs, ns, sgsh, qg):
    dma = pltpu.SemaphoreType.DMA
    return pl.pallas_call(
        functools.partial(exchange_kernel, n, seqs),
        out_shape=(
            jax.ShapeDtypeStruct(hs.shape[1:], BF),
            jax.ShapeDtypeStruct(ns.shape[1:], BF),
            jax.ShapeDtypeStruct((seqs,) + sgsh.shape, BF),
            jax.ShapeDtypeStruct((seqs,) + qg.shape, BF),
        ),
        in_specs=[VMEM] * 4,
        out_specs=(VMEM,) * 4,
        scratch_shapes=[
            pltpu.VMEM(hs.shape, BF), pltpu.VMEM(ns.shape, BF),
            dma((n,)), dma((n,)), dma((n,)), dma((n,)),
            dma((2, seqs - 1, 2)), dma((2, seqs - 1, 2)),
        ],
        compiler_params=pltpu.CompilerParams(
            collective_id=1, has_side_effects=True, vmem_limit_bytes=LIMIT
        ),
        name="exchange",
    )(hs, ns, sgsh, qg)


def weight_kernel(spans, seqs, sgsh, q, og, picks, wk, wv):
    reach = sgsh.shape[-1]
    for lane, right, out in ((0, q, wk), (1, og, wv)):
        total = jnp.zeros(out.shape, F32)
        for s in range(seqs):
            for u in range(spans):
                here = pl.ds(u * SPAN, SPAN if u < spans - 1 else TAIL)
                grad = contract_rows(sgsh[s, lane, 0, here, :], right[s, here, :]).astype(BF)
                total += contract_rows(picks[s, pl.ds(u * reach, reach), :], grad)
        out[...] = total


def weights(spans, sgsh, q, og, picks):
    seqs, _, heads, rows, reach = sgsh.shape
    cols = picks.shape[2]
    narrow = pl.BlockSpec((seqs, rows, HS), lambda h: (0, 0, h))
    result = jax.ShapeDtypeStruct((cols, heads * HS), F32)
    return pl.pallas_call(
        functools.partial(weight_kernel, spans, seqs),
        grid=(heads,),
        out_shape=(result, result),
        in_specs=[
            pl.BlockSpec((seqs, 2, 1, rows, reach), lambda h: (0, 0, h, 0, 0)),
            narrow, narrow,
            pl.BlockSpec(picks.shape, lambda h: (0, 0, 0)),
        ],
        out_specs=(pl.BlockSpec((cols, HS), lambda h: (0, h)),) * 2,
        compiler_params=pltpu.CompilerParams(vmem_limit_bytes=LIMIT),
        name="weights",
    )(sgsh, q, og, picks)


def body(n, seqs, hidden, neighbours, slot_of, w_query, w_key, w_value, out_grad):
    width = w_query.shape[1]
    length = hidden.shape[1]
    slot_count = neighbours.shape[1]
    spans = slot_of.shape[1]
    lag = SPAN - 1
    rows = (spans - 1) * SPAN + TAIL
    slots = slot_of[0].reshape(-1)

    def later(x):
        return jnp.pad(x[lag:], ((0, rows - (length - lag)), (0, 0)))

    def back(x):
        return jnp.pad(x[: length - lag], ((lag, 0), (0, 0)))[None]

    og = later(out_grad[0])
    row = lax.axis_index("seq")
    whole, every, qall, ogall = gather(
        n, seqs, later(hidden[0]), neighbours[0].reshape(slot_count * R, DE), og, w_query
    )
    states = jnp.take(every.reshape(-1, R, DE), slots, axis=0).reshape(-1, DE)
    tokens_all = lax.all_to_all(
        whole.reshape((seqs, n // seqs) + whole.shape[1:]), "seq", 0, 0, tiled=True
    )
    picks = lax.all_to_all(
        states.reshape(-1, seqs, DE // seqs).transpose(1, 0, 2), "seq", 0, 0, tiled=True
    )
    keys = jnp.dot(states, w_key, preferred_element_type=F32).astype(BF)
    values = jnp.dot(states, w_value, preferred_element_type=F32).astype(BF)
    query = lax.dynamic_index_in_dim(qall, row, 0, keepdims=False)
    mixed, qg, kg, vg, sgsh = attention(spans, query, og, keys, values)
    feature_terms = lax.dot_general(
        w_query.reshape(n, -1, width), qg, (((2,), (1,)), ((), ())), preferred_element_type=F32
    ).astype(BF)
    feature_terms = feature_terms.transpose(0, 2, 1)
    terms = (contract_cols(kg, w_key) + contract_cols(vg, w_value)).astype(BF)
    terms = jnp.concatenate([terms.reshape(-1, R, DE), jnp.zeros((1, R, DE), BF)], 0)
    wanted = lax.iota(jnp.int32, slot_count * n)[:, None] == slots[None, :]
    place = jnp.where(wanted.any(1), jnp.argmax(wanted, 1).astype(jnp.int32), slots.shape[0])
    placed = jnp.take(terms, place, axis=0).reshape(n, slot_count * R, DE)
    hid, nbr, zall, qgall = exchange(n, seqs, feature_terms, placed, sgsh, qg)
    query_part = lax.dot_general(
        tokens_all.transpose(1, 3, 0, 2).reshape(-1, seqs * rows),
        qgall.reshape(seqs * rows, width),
        (((1,), (0,)), ((), ())),
        preferred_element_type=F32,
    )
    wk, wv = weights(spans, zall, qall, ogall, picks)
    return (
        back(mixed), back(hid), nbr.reshape(1, slot_count, R, DE), query_part, wk, wv
    )


def solution(mesh):
    return jax.shard_map(
        functools.partial(body, mesh.shape["tensor"], mesh.shape["seq"]),
        mesh=mesh,
        in_specs=(
            P("seq", None, "tensor"),
            P("seq", "tensor", None, None),
            P("seq", None, None),
            P(None, "tensor"),
            P(None, "tensor"),
            P(None, "tensor"),
            P("seq", None, "tensor"),
        ),
        out_specs=(
            P("seq", None, "tensor"),
            P("seq", None, "tensor"),
            P("seq", "tensor", None, None),
            P("seq", "tensor"),
            P("seq", "tensor"),
            P("seq", "tensor"),
        ),
        check_vma=False,
    )
```

```python
import functools
import math

import jax
import jax.numpy as jnp
from jax import lax
from jax.experimental import pallas as pl
from jax.experimental.pallas import tpu as pltpu
from jax.sharding import PartitionSpec as P

HS = 128
DE = 1024
SPAN = 64
R = 128
TAIL = 16
MESH = pl.DeviceIdType.MESH
BF = jnp.bfloat16
F32 = jnp.float32
VMEM = pl.BlockSpec(memory_space=pltpu.VMEM)
ANY = pl.BlockSpec(memory_space=pl.ANY)
LIMIT = 60 * 2**20
TILE = 256


def contract_rows(left, right):
    return lax.dot_general(left, right, (((0,), (0,)), ((), ())), preferred_element_type=F32)


def contract_cols(left, right):
    return lax.dot_general(left, right, (((1,), (1,)), ((), ())), preferred_element_type=F32)


def remote(src, dst, send, recv, axis, index):
    return pltpu.make_async_remote_copy(
        src_ref=src, dst_ref=dst, send_sem=send, recv_sem=recv,
        device_id={axis: index}, device_id_type=MESH,
    )


def gather_kernel(
    n, seqs, slots, hid, nb, og, w_hbm, wk_hbm, wv_hbm, qall, ogall, query, keys, values, ext,
    w, wk, wv, acc, whole, every, states, w_sem, h_send, h_recv, n_send, n_recv, z_send, z_recv,
):
    me = lax.axis_index("tensor")
    row = lax.axis_index("seq")
    chips = n // 2
    core = lax.rem(me, 2)
    chip = me // 2
    twin = me + 1 - 2 * core
    rows, depth = hid.shape
    many, wide = states.shape
    share, cut = many // n, wide // seqs
    pieces = n * depth // seqs // cut

    def peer(k):
        return lax.rem(chip + k, chips) * 2 + core

    def over(k):
        return lax.rem(row + k, seqs)

    fetches = [
        pltpu.make_async_copy(src, dst, w_sem.at[i])
        for i, (src, dst) in enumerate(((w_hbm, w), (wk_hbm, wk), (wv_hbm, wv)))
    ]
    for fetch in fetches:
        fetch.start()
    barrier = pltpu.get_barrier_semaphore()
    pl.semaphore_signal(barrier, inc=1, device_id={"tensor": twin}, device_id_type=MESH)

    @pl.loop(1, chips)
    def _(k):
        pl.semaphore_signal(barrier, inc=1, device_id={"tensor": peer(k)}, device_id_type=MESH)

    for k in range(1, seqs):
        pl.semaphore_signal(barrier, inc=1, device_id={"seq": over(k)}, device_id_type=MESH)
    pl.semaphore_wait(barrier, chips + seqs - 1)

    def own(ref, out, send, recv, k, target):
        return remote(ref, out.at[me], send.at[k], recv.at[me], "tensor", target)

    def onward(out, send, recv, k):
        return remote(
            out.at[peer(k)], out.at[peer(k)], send.at[chips + k], recv.at[peer(k)], "tensor", twin
        )

    def arrival(out, send, recv, index):
        return remote(out.at[index], out.at[index], send.at[0], recv.at[index], "tensor", twin)

    def z_copy(ref, out, lane, k):
        return remote(ref, out.at[row], z_send.at[lane, k], z_recv.at[lane, row], "seq", over(k))

    def token_part(dest):
        at = (dest * pieces + me) * cut
        return at // depth, pl.ds(pl.multiple_of(lax.rem(at, depth), cut), cut)

    def state_part(dest):
        return (
            pl.ds(pl.multiple_of(me * share, share), share),
            pl.ds(pl.multiple_of(dest * cut, cut), cut),
        )

    def token_copy(k):
        block, cols = token_part(over(k))
        return remote(
            whole.at[block, :, cols], ext.at[row, pl.ds(0, rows)],
            z_send.at[2, k], z_recv.at[2, row], "seq", over(k),
        )

    def state_copy(k):
        here, cols = state_part(over(k))
        return remote(
            states.at[here, cols], ext.at[row, pl.ds(rows, share)],
            z_send.at[3, k], z_recv.at[3, row], "seq", over(k),
        )

    @pl.loop(1, chips)
    def _(k):
        own(hid, whole, h_send, h_recv, k, peer(k)).start()

    own(hid, whole, h_send, h_recv, 0, twin).start()

    @pl.loop(1, chips)
    def _(k):
        own(nb, every, n_send, n_recv, k, peer(k)).start()

    own(nb, every, n_send, n_recv, 0, twin).start()
    for k in range(1, seqs):
        z_copy(og, ogall, 0, k).start()
    whole[me] = hid[...]
    every[me] = nb[...]
    ogall[row] = og[...]
    fetches[0].wait()

    def add(index):
        part = w[pl.ds(pl.multiple_of(index * depth, depth), depth), :]
        acc[...] += jnp.dot(whole[index], part, preferred_element_type=F32)

    acc[...] = jnp.zeros_like(acc)
    add(me)

    @pl.loop(1, chips)
    def _(k):
        arrival(whole, h_send, h_recv, peer(k)).wait_recv()
        onward(whole, h_send, h_recv, k).start()
        add(peer(k))

    @pl.loop(0, chips)
    def _(k):
        index = peer(k) + 1 - 2 * core
        arrival(whole, h_send, h_recv, index).wait_recv()
        add(index)

    @pl.when(me < pieces)
    def _():
        for k in range(1, seqs):
            token_copy(k).start()
        block, cols = token_part(row)
        ext[row, pl.ds(0, rows), :] = whole[block, :, cols]

    query[...] = acc[...].astype(BF)
    qall[row] = query[...]
    for k in range(1, seqs):
        z_copy(qall.at[row], qall, 1, k).start()

    @pl.loop(1, chips)
    def _(k):
        arrival(every, n_send, n_recv, peer(k)).wait_recv()
        onward(every, n_send, n_recv, k).start()

    @pl.loop(0, chips)
    def _(k):
        arrival(every, n_send, n_recv, peer(k) + 1 - 2 * core).wait_recv()

    held = every.shape[1]
    for i in range(many // R):
        slot = slots[i]
        block = every[slot, 0] if held == 1 else every[slot // held, slot % held]
        states[pl.ds(i * R, R), :] = block
    for k in range(1, seqs):
        state_copy(k).start()
    here, cols = state_part(row)
    ext[row, pl.ds(rows, share), :] = states[here, cols]
    for fetch in fetches[1:]:
        fetch.wait()

    @pl.loop(0, wk.shape[1] // TILE)
    def _(i):
        at = pl.ds(pl.multiple_of(i * TILE, TILE), TILE)
        keys[:, at] = jnp.dot(states[...], wk[:, at], preferred_element_type=F32).astype(BF)
        values[:, at] = jnp.dot(states[...], wv[:, at], preferred_element_type=F32).astype(BF)

    for k in range(1, seqs):
        came = over(k)
        for lane, out in ((0, ogall), (1, qall)):
            remote(
                out.at[came], out.at[came], z_send.at[lane, 0], z_recv.at[lane, came], "seq", came
            ).wait_recv()
            z_copy(og if lane == 0 else qall.at[row], out, lane, k).wait_send()
        remote(
            ext.at[came, pl.ds(rows, share)], ext.at[came, pl.ds(rows, share)],
            z_send.at[3, 0], z_recv.at[3, came], "seq", came,
        ).wait_recv()
        state_copy(k).wait_send()

        @pl.when(me < pieces)
        def _():
            remote(
                ext.at[came, pl.ds(0, rows)], ext.at[came, pl.ds(0, rows)],
                z_send.at[2, 0], z_recv.at[2, came], "seq", came,
            ).wait_recv()
            token_copy(k).wait_send()

    for ref, out, send, recv in ((hid, whole, h_send, h_recv), (nb, every, n_send, n_recv)):
        own(ref, out, send, recv, 0, twin).wait_send()

        @pl.loop(1, chips)
        def _(k):
            own(ref, out, send, recv, k, peer(k)).wait_send()
            onward(out, send, recv, k).wait_send()


def gather(n, seqs, slots, hid, nb, og, w_query, w_key, w_value):
    rows, depth = hid.shape
    width = w_query.shape[1]
    many = slots.shape[0] * R
    dma = pltpu.SemaphoreType.DMA
    return pl.pallas_call(
        functools.partial(gather_kernel, n, seqs),
        out_shape=(
            jax.ShapeDtypeStruct((seqs, rows, width), BF),
            jax.ShapeDtypeStruct((seqs, rows, width), BF),
            jax.ShapeDtypeStruct((rows, width), BF),
            jax.ShapeDtypeStruct((many, width), BF),
            jax.ShapeDtypeStruct((many, width), BF),
            jax.ShapeDtypeStruct((seqs, rows + many // n, DE // seqs), BF),
        ),
        in_specs=[pl.BlockSpec(memory_space=pltpu.SMEM), VMEM, VMEM, VMEM, ANY, ANY, ANY],
        out_specs=(VMEM,) * 6,
        scratch_shapes=[
            pltpu.VMEM(w_query.shape, BF),
            pltpu.VMEM(w_key.shape, BF),
            pltpu.VMEM(w_value.shape, BF),
            pltpu.VMEM((rows, width), F32),
            pltpu.VMEM((n, rows, depth), BF),
            pltpu.VMEM((n,) + nb.shape, BF),
            pltpu.VMEM((many, DE), BF),
            dma((3,)), dma((n,)), dma((n,)), dma((n,)), dma((n,)), dma((4, seqs)), dma((4, seqs)),
        ],
        compiler_params=pltpu.CompilerParams(
            collective_id=0, has_side_effects=True, vmem_limit_bytes=LIMIT
        ),
        name="gather",
    )(slots, hid, nb, og, w_query, w_key, w_value)


def attention_kernel(spans, q, og, key, value, mixed, qg, kg, vg, sgsh):
    scale = 1.0 / math.sqrt(HS)
    reach = key.shape[0] // spans
    for u in range(spans):
        here = pl.ds(u * SPAN, SPAN if u < spans - 1 else TAIL)
        rows = pl.ds(u * reach, reach)
        qu, gu, ku, vu = q[here, :], og[here, :], key[rows, :], value[rows, :]
        raised = jnp.exp(contract_cols(qu, ku) * scale)
        shares = raised / jnp.sum(raised, axis=-1, keepdims=True)
        share_bf = shares.astype(BF)
        mixed[here, :] = jnp.dot(share_bf, vu, preferred_element_type=F32).astype(BF)
        share_grad = contract_cols(gu, vu)
        centre = jnp.sum(shares * share_grad, axis=-1, keepdims=True)
        score_grad = (shares * (share_grad - centre) * scale).astype(BF)
        qg[here, :] = jnp.dot(score_grad, ku, preferred_element_type=F32).astype(BF)
        kg[rows, :] = contract_rows(score_grad, qu).astype(BF)
        vg[rows, :] = contract_rows(share_bf, gu).astype(BF)
        sgsh[0, 0, here, :] = score_grad
        sgsh[1, 0, here, :] = share_bf


def attention(spans, q, og, keys, values):
    rows, width = q.shape
    heads = width // HS
    many = keys.shape[0]
    narrow = pl.BlockSpec((rows, HS), lambda h: (0, h))
    tall = pl.BlockSpec((many, HS), lambda h: (0, h))
    reach = many // spans
    return pl.pallas_call(
        functools.partial(attention_kernel, spans),
        grid=(heads,),
        out_shape=(
            jax.ShapeDtypeStruct((rows, width), BF),
            jax.ShapeDtypeStruct((rows, width), BF),
            jax.ShapeDtypeStruct((many, width), BF),
            jax.ShapeDtypeStruct((many, width), BF),
            jax.ShapeDtypeStruct((2, heads, rows, reach), BF),
        ),
        in_specs=[narrow, narrow, tall, tall],
        out_specs=(
            narrow, narrow, tall, tall,
            pl.BlockSpec((2, 1, rows, reach), lambda h: (0, h, 0, 0)),
        ),
        compiler_params=pltpu.CompilerParams(vmem_limit_bytes=LIMIT),
        name="attention",
    )(q, og, keys, values)


def exchange_kernel(
    n, seqs, spans, place, sgsh, qg, kg, vg, q, og, ext, w_hbm, wk_hbm, wv_hbm,
    hid, nbr, qgall, extall, gk, gv,
    w, wk, wv, hs, ns, h_in, n_in, terms, zall, prow, picks, kbuf, vbuf,
    w_sem, p_sem, h_send, h_recv, n_send, n_recv, e_send, e_recv, z_send, z_recv,
):
    me = lax.axis_index("tensor")
    row = lax.axis_index("seq")
    chips = n // 2
    core = lax.rem(me, 2)
    chip = me // 2
    twin = me + 1 - 2 * core
    rows, width = qg.shape
    many = kg.shape[0]
    share, reach = many // n, many // spans
    depth = hs.shape[2]
    held = ns.shape[1]

    def peer(k):
        return lax.rem(me + k, n)

    def mate(k):
        return lax.rem(chip + k, chips) * 2 + core

    def tile(i, size=TILE):
        return pl.ds(pl.multiple_of(i * size, size), size)

    fetches = [
        pltpu.make_async_copy(src, dst, w_sem.at[i])
        for i, (src, dst) in enumerate(((wk_hbm, wk), (wv_hbm, wv), (w_hbm, w)))
    ]
    for fetch in fetches:
        fetch.start()
    barrier = pltpu.get_barrier_semaphore()

    @pl.loop(1, n)
    def _(k):
        pl.semaphore_signal(barrier, inc=1, device_id={"tensor": peer(k)}, device_id_type=MESH)

    for k in range(1, seqs):
        pl.semaphore_signal(
            barrier, inc=1, device_id={"seq": lax.rem(row + k, seqs)}, device_id_type=MESH
        )
    pl.semaphore_wait(barrier, n - 1 + seqs - 1)

    def scatter(ref, into, send, recv, k):
        return remote(ref.at[peer(k)], into.at[me], send.at[k], recv.at[me], "tensor", peer(k))

    def spread(k):
        return remote(
            ext, extall.at[me], e_send.at[k], e_recv.at[me], "tensor", mate(k)
        )

    def to_twin():
        return remote(ext, extall.at[me], e_send.at[0], e_recv.at[me], "tensor", twin)

    def onward(k):
        return remote(
            extall.at[mate(k)], extall.at[mate(k)], e_send.at[chips + k], e_recv.at[mate(k)],
            "tensor", twin,
        )

    def came(index):
        return remote(
            extall.at[index], extall.at[index], e_send.at[0], e_recv.at[index], "tensor", twin
        )

    outs = (zall, qgall)
    owns = (sgsh, qg)

    def hop(side, h, lane):
        step = 1 - 2 * side
        origin = row - step * h
        src = owns[lane] if h == 0 else outs[lane].at[origin]
        return remote(
            src, outs[lane].at[origin], z_send.at[side, h, lane], z_recv.at[side, h, lane],
            "seq", row + step,
        )

    def sends(side, h):
        if side == 0:
            return (row - h >= 0) & (row + 1 < seqs)
        return (row + h < seqs) & (row >= 1)

    def arrives(side, h):
        return row - 1 - h >= 0 if side == 0 else row + 1 + h < seqs

    def arrived(side, h, lane):
        step = 1 - 2 * side
        origin = row - step * (h + 1)
        return remote(
            outs[lane].at[origin], outs[lane].at[origin],
            z_send.at[side, h, lane], z_recv.at[side, h, lane], "seq", row - step,
        )

    for side in range(2):
        @pl.when(sends(side, 0))
        def _():
            for lane in range(2):
                hop(side, 0, lane).start()

    @pl.loop(1, chips)
    def _(k):
        spread(k).start()

    to_twin().start()
    mine = pltpu.make_async_copy(ext, extall.at[me], p_sem.at[n])
    mine.start()
    qgall[row] = qg[...]

    fetches[0].wait()
    fetches[1].wait()

    @pl.loop(0, wk.shape[0] // TILE)
    def _(i):
        part = contract_cols(kg[...], wk[tile(i), :]) + contract_cols(vg[...], wv[tile(i), :])
        for p in range(many // R):
            terms[p, :, tile(i)] = part[p * R:(p + 1) * R].astype(BF)

    terms[many // R] = jnp.zeros_like(terms[0])

    @pl.loop(0, n)
    def _(k):
        for j in range(held):
            ns[peer(k), j] = terms[place[peer(k) * held + j]]

    @pl.loop(1, n)
    def _(k):
        scatter(ns, n_in, n_send, n_recv, k).start()

    @pl.loop(1, chips)
    def _(k):
        came(mate(k)).wait_recv()
        onward(k).start()

    fetches[2].wait()

    def hidden_term(index):
        hs[index] = contract_cols(qg[...], w[tile(index, depth), :]).astype(BF)

    @pl.loop(1, n)
    def _(k):
        hidden_term(peer(k))
        scatter(hs, h_in, h_send, h_recv, k).start()

    hidden_term(me)

    @pl.loop(0, chips)
    def _(k):
        came(mate(k) + 1 - 2 * core).wait_recv()

    mine.wait()

    def pick_copy(t):
        at = pl.ds(pl.multiple_of(t * share, share), share)
        return pltpu.make_async_copy(
            extall.at[t, :, pl.ds(rows, share)], prow.at[:, at], p_sem.at[t]
        )

    @pl.loop(0, n)
    def _(t):
        pick_copy(t).start()

    @pl.loop(0, n)
    def _(t):
        pick_copy(t).wait()

    def add(origin, key_ref, value_ref):
        picks[...] = prow[origin].T

        @pl.loop(0, width // TILE)
        def _(i):
            gk[:, tile(i)] += jnp.dot(picks[...], key_ref[:, tile(i)], preferred_element_type=F32)
            gv[:, tile(i)] += jnp.dot(picks[...], value_ref[:, tile(i)], preferred_element_type=F32)

    def rebuild(origin):
        @pl.loop(0, width // HS)
        def _(h):
            for lane, right, out in ((0, q, kbuf), (1, og, vbuf)):
                for u in range(spans):
                    here = pl.ds(u * SPAN, SPAN if u < spans - 1 else TAIL)
                    out[pl.ds(u * reach, reach), tile(h, HS)] = contract_rows(
                        zall[origin, lane, h, here, :], right[origin, here, tile(h, HS)]
                    ).astype(BF)

        add(origin, kbuf, vbuf)

    gk[...] = jnp.zeros_like(gk)
    gv[...] = jnp.zeros_like(gv)
    add(row, kg, vg)
    for h in range(seqs - 1):
        for lane in range(2):
            for side in range(2):
                @pl.when(arrives(side, h))
                def _():
                    arrived(side, h, lane).wait_recv()

                if h + 1 < seqs - 1:
                    @pl.when(sends(side, h + 1))
                    def _():
                        hop(side, h + 1, lane).start()

        for side in range(2):
            @pl.when(arrives(side, h))
            def _():
                rebuild(row - (1 - 2 * side) * (h + 1))

    for ref, into, send, recv, out in (
        (ns, n_in, n_send, n_recv, nbr), (hs, h_in, h_send, h_recv, hid)
    ):
        @pl.loop(1, n)
        def _(k):
            remote(
                into.at[peer(k)], into.at[peer(k)], send.at[0], recv.at[peer(k)],
                "tensor", peer(k),
            ).wait_recv()

        into[me] = ref[me]
        total = into[0].astype(F32)
        for j in range(1, n):
            total = total + into[j].astype(F32)
        out[...] = total.astype(BF)

    for side in range(2):
        for h in range(seqs - 1):
            @pl.when(sends(side, h))
            def _():
                for lane in range(2):
                    hop(side, h, lane).wait_send()

    to_twin().wait_send()

    @pl.loop(1, chips)
    def _(k):
        spread(k).wait_send()
        onward(k).wait_send()

    @pl.loop(1, n)
    def _(k):
        scatter(hs, h_in, h_send, h_recv, k).wait_send()
        scatter(ns, n_in, n_send, n_recv, k).wait_send()


def exchange(n, seqs, spans, held, place, sgsh, qg, kg, vg, q, og, ext, w_query, w_key, w_value):
    dma = pltpu.SemaphoreType.DMA
    rows, width = qg.shape
    many = kg.shape[0]
    depth = w_query.shape[0] // n
    cut = DE // seqs
    return pl.pallas_call(
        functools.partial(exchange_kernel, n, seqs, spans),
        out_shape=(
            jax.ShapeDtypeStruct((rows, depth), BF),
            jax.ShapeDtypeStruct((held, R, DE), BF),
            jax.ShapeDtypeStruct((seqs, rows, width), BF),
            jax.ShapeDtypeStruct((n,) + ext.shape, BF),
            jax.ShapeDtypeStruct((cut, width), F32),
            jax.ShapeDtypeStruct((cut, width), F32),
        ),
        in_specs=[pl.BlockSpec(memory_space=pltpu.SMEM)] + [VMEM] * 7 + [ANY] * 3,
        out_specs=(VMEM, VMEM, VMEM, ANY, VMEM, VMEM),
        scratch_shapes=[
            pltpu.VMEM(w_query.shape, BF),
            pltpu.VMEM(w_key.shape, BF),
            pltpu.VMEM(w_value.shape, BF),
            pltpu.VMEM((n, rows, depth), BF),
            pltpu.VMEM((n, held, R, DE), BF),
            pltpu.VMEM((n, rows, depth), BF),
            pltpu.VMEM((n, held, R, DE), BF),
            pltpu.VMEM((many // R + 1, R, DE), BF),
            pltpu.VMEM((seqs,) + sgsh.shape, BF),
            pltpu.VMEM((seqs, many, cut), BF),
            pltpu.VMEM((cut, many), BF),
            pltpu.VMEM((many, width), BF),
            pltpu.VMEM((many, width), BF),
            dma((3,)), dma((n + 1,)),
            dma((n,)), dma((n,)), dma((n,)), dma((n,)), dma((n,)), dma((n,)),
            dma((2, seqs - 1, 2)), dma((2, seqs - 1, 2)),
        ],
        compiler_params=pltpu.CompilerParams(
            collective_id=1, has_side_effects=True, vmem_limit_bytes=LIMIT
        ),
        name="exchange",
    )(place, sgsh, qg, kg, vg, q, og, ext, w_query, w_key, w_value)


def body(n, seqs, hidden, neighbours, slot_of, w_query, w_key, w_value, out_grad):
    width = w_query.shape[1]
    length = hidden.shape[1]
    slot_count = neighbours.shape[1]
    spans = slot_of.shape[1]
    lag = SPAN - 1
    rows = (spans - 1) * SPAN + TAIL
    slots = slot_of[0].reshape(-1)

    def later(x):
        return jnp.pad(x[lag:], ((0, rows - (length - lag)), (0, 0)))

    def back(x):
        return jnp.pad(x[: length - lag], ((lag, 0), (0, 0)))[None]

    og = later(out_grad[0])
    qall, ogall, query, keys, values, ext = gather(
        n, seqs, slots, later(hidden[0]), neighbours[0], og, w_query, w_key, w_value
    )
    mixed, qg, kg, vg, sgsh = attention(spans, query, og, keys, values)
    wanted = lax.iota(jnp.int32, slot_count * n)[:, None] == slots[None, :]
    nth = lax.iota(jnp.int32, slots.shape[0])[None, :] - slots.shape[0]
    place = jnp.sum(jnp.where(wanted, nth, 0), 1) + slots.shape[0]
    hid, nbr, qgall, extall, wk, wv = exchange(
        n, seqs, spans, slot_count, place, sgsh, qg, kg, vg, qall, ogall, ext,
        w_query, w_key, w_value,
    )
    pieces = w_query.shape[0] // seqs // ext.shape[2]
    query_part = lax.dot_general(
        extall[:pieces, :, :rows].transpose(0, 3, 1, 2).reshape(-1, seqs * rows),
        qgall.reshape(seqs * rows, width),
        (((1,), (0,)), ((), ())),
        preferred_element_type=F32,
    )
    return (back(mixed), back(hid), nbr[None], query_part, wk, wv)


def solution(mesh):
    return jax.shard_map(
        functools.partial(body, mesh.shape["tensor"], mesh.shape["seq"]),
        mesh=mesh,
        in_specs=(
            P("seq", None, "tensor"),
            P("seq", "tensor", None, None),
            P("seq", None, None),
            P(None, "tensor"),
            P(None, "tensor"),
            P(None, "tensor"),
            P("seq", None, "tensor"),
        ),
        out_specs=(
            P("seq", None, "tensor"),
            P("seq", None, "tensor"),
            P("seq", "tensor", None, None),
            P("seq", "tensor"),
            P("seq", "tensor"),
            P("seq", "tensor"),
        ),
        check_vma=False,
    )
```

```python
import functools
import math

import jax
import jax.numpy as jnp
from jax import lax
from jax.experimental import pallas as pl
from jax.experimental.pallas import tpu as pltpu
from jax.sharding import PartitionSpec as P

HS = 128
DE = 1024
SPAN = 64
R = 128
TAIL = 16
MESH = pl.DeviceIdType.MESH
BF = jnp.bfloat16
F32 = jnp.float32
VMEM = pl.BlockSpec(memory_space=pltpu.VMEM)
ANY = pl.BlockSpec(memory_space=pl.ANY)
LIMIT = 63 * 2**20
TILE = 256


def contract_rows(left, right):
    return lax.dot_general(left, right, (((0,), (0,)), ((), ())), preferred_element_type=F32)


def contract_cols(left, right):
    return lax.dot_general(left, right, (((1,), (1,)), ((), ())), preferred_element_type=F32)


def remote(src, dst, send, recv, axis, index):
    return pltpu.make_async_remote_copy(
        src_ref=src, dst_ref=dst, send_sem=send, recv_sem=recv,
        device_id={axis: index}, device_id_type=MESH,
    )


def kernel(
    n, seqs, spans, slots, hid_in, nb, og_in, w_hbm, wk_hbm, wv_hbm,
    mixed, hid_out, nbr, qgall, extall, gk, gv,
    w, wk, wv, acc, hid, whole, every, states, keys, values, kg, vg, qall, ogall, ext,
    h_in, n_in, terms, zall, picks,
    w_sem, p_sem, h_send, h_recv, n_send, n_recv, z_send, z_recv,
    e_send, e_recv, hs_send, hs_recv, ns_send, ns_recv, line_send, line_recv,
):
    me = lax.axis_index("tensor")
    row = lax.axis_index("seq")
    chips = n // 2
    core = lax.rem(me, 2)
    chip = me // 2
    twin = me + 1 - 2 * core
    rows, depth = hid.shape
    _, many, cut = states.shape
    width = acc.shape[1]
    heads = width // HS
    share, reach = many // n, many // spans
    pieces = n * depth // seqs // cut
    blocks = many // R
    held = every.shape[1]
    near = slots.shape[1]
    scale = 1.0 / math.sqrt(HS)

    def mate(k):
        return lax.rem(chip + k, chips) * 2 + core

    def peer(k):
        return lax.rem(me + k, n)

    def over(k):
        return lax.rem(row + k, seqs)

    def tile(i, size=TILE):
        return pl.ds(pl.multiple_of(i * size, size), size)

    def slot_at(i):
        return slots[i // near, i % near]

    fetches = [
        pltpu.make_async_copy(src, dst, w_sem.at[i])
        for i, (src, dst) in enumerate(((w_hbm, w), (wk_hbm, wk), (wv_hbm, wv)))
    ]
    for fetch in fetches:
        fetch.start()
    barrier = pltpu.get_barrier_semaphore()

    @pl.loop(1, n)
    def _(k):
        pl.semaphore_signal(barrier, inc=1, device_id={"tensor": peer(k)}, device_id_type=MESH)

    for k in range(1, seqs):
        pl.semaphore_signal(barrier, inc=1, device_id={"seq": over(k)}, device_id_type=MESH)

    length = hid_in.shape[0]
    for ref, out in ((hid_in, hid), (og_in, ogall.at[row])):
        whole_rows = ref[pl.ds(length - rows, rows), :].astype(F32)
        moved = pltpu.roll(whole_rows, rows - (SPAN - 1 - (length - rows)), 0)
        at = lax.broadcasted_iota(jnp.int32, moved.shape, 0)
        out[...] = jnp.where(at < length - SPAN + 1, moved, 0.0).astype(BF)
    pl.semaphore_wait(barrier, n - 1 + seqs - 1)

    def own(ref, out, send, recv, k, target):
        return remote(ref, out.at[me], send.at[k], recv.at[me], "tensor", target)

    def onward(out, send, recv, k):
        return remote(
            out.at[mate(k)], out.at[mate(k)], send.at[chips + k], recv.at[mate(k)], "tensor", twin
        )

    def arrival(out, send, recv, index):
        return remote(out.at[index], out.at[index], send.at[0], recv.at[index], "tensor", twin)

    def spread(ref, out, send, recv):
        @pl.loop(1, chips)
        def _(k):
            own(ref, out, send, recv, k, mate(k)).start()

        own(ref, out, send, recv, 0, twin).start()

    def pass_on(out, send, recv, use=None):
        @pl.loop(1, chips)
        def _(k):
            arrival(out, send, recv, mate(k)).wait_recv()
            onward(out, send, recv, k).start()
            if use is not None:
                use(mate(k))

    def rest(out, send, recv, use=None):
        @pl.loop(0, chips)
        def _(k):
            index = mate(k) + 1 - 2 * core
            arrival(out, send, recv, index).wait_recv()
            if use is not None:
                use(index)

    def sent(ref, out, send, recv):
        own(ref, out, send, recv, 0, twin).wait_send()

        @pl.loop(1, chips)
        def _(k):
            own(ref, out, send, recv, k, mate(k)).wait_send()
            onward(out, send, recv, k).wait_send()

    def z_copy(out, lane, k):
        return remote(
            out.at[row], out.at[row], z_send.at[lane, k], z_recv.at[lane, row], "seq", over(k)
        )

    def token_part(dest):
        at = (dest * pieces + me) * cut
        return at // depth, pl.ds(pl.multiple_of(lax.rem(at, depth), cut), cut)

    def state_part(dest):
        return dest, tile(me, share)

    def token_copy(k):
        block, cols = token_part(over(k))
        return remote(
            whole.at[block, :, cols], ext.at[row, pl.ds(0, rows)],
            z_send.at[2, k], z_recv.at[2, row], "seq", over(k),
        )

    def state_copy(k):
        return remote(
            states.at[state_part(over(k))], ext.at[row, pl.ds(rows, share)],
            z_send.at[3, k], z_recv.at[3, row], "seq", over(k),
        )

    def z_came(ref, lane, index):
        return remote(ref, ref, z_send.at[lane, 0], z_recv.at[lane, index], "seq", index)

    spread(hid, whole, h_send, h_recv)
    spread(nb, every, n_send, n_recv)
    for k in range(1, seqs):
        z_copy(ogall, 0, k).start()
    whole[me] = hid[...]
    every[me] = nb[...]
    fetches[0].wait()

    def project(index):
        acc[...] += jnp.dot(whole[index], w[tile(index, depth), :], preferred_element_type=F32)

    acc[...] = jnp.zeros_like(acc)
    project(me)
    pass_on(whole, h_send, h_recv, project)
    rest(whole, h_send, h_recv, project)

    @pl.when(me < pieces)
    def _():
        for k in range(1, seqs):
            token_copy(k).start()
        block, cols = token_part(row)
        ext[row, pl.ds(0, rows), :] = whole[block, :, cols]

    qall[row] = acc[...].astype(BF)
    pass_on(every, n_send, n_recv)
    rest(every, n_send, n_recv)
    for i in range(blocks):
        slot = slot_at(i)
        block = every[slot, 0] if held == 1 else every[slot // held, slot % held]
        for part in range(seqs):
            states[part, pl.ds(i * R, R), :] = block[:, part * cut:(part + 1) * cut]
    for k in range(1, seqs):
        state_copy(k).start()
    for k in range(1, seqs):
        z_copy(qall, 1, k).start()
    ext[row, pl.ds(rows, share), :] = states[row, tile(me, share), :]
    for fetch in fetches[1:]:
        fetch.wait()

    @pl.loop(0, width // TILE)
    def _(i):
        for out, weight in ((keys, wk), (values, wv)):
            total = jnp.zeros((many, TILE), F32)
            for part in range(seqs):
                total += jnp.dot(
                    states[part], weight[pl.ds(part * cut, cut), tile(i)],
                    preferred_element_type=F32,
                )
            out[:, tile(i)] = total.astype(BF)

    def lane_ref(origin, lane):
        if isinstance(lane, int) and lane == heads:
            return qgall.at[origin]
        return zall.at[origin, lane]

    def hop(side, h, lane):
        step = 1 - 2 * side
        ref = lane_ref(row - step * h, lane)
        return remote(
            ref, ref, line_send.at[side, h, lane], line_recv.at[side, h, lane], "seq", row + step
        )

    def sends(side, h):
        if side == 0:
            return (row - h >= 0) & (row + 1 < seqs)
        return (row + h < seqs) & (row >= 1)

    def arrives(side, h):
        return row - 1 - h >= 0 if side == 0 else row + 1 + h < seqs

    def arrived(side, h, lane):
        step = 1 - 2 * side
        ref = lane_ref(row - step * (h + 1), lane)
        return remote(
            ref, ref, line_send.at[side, h, lane], line_recv.at[side, h, lane], "seq", row - step
        )

    def push(lane):
        for side in range(2):
            @pl.when(sends(side, 0))
            def _():
                hop(side, 0, lane).start()

    def relay(h, lane):
        for side in range(2):
            @pl.when(arrives(side, h))
            def _():
                arrived(side, h, lane).wait_recv()

            if h + 1 < seqs - 1:
                @pl.when(sends(side, h + 1))
                def _():
                    hop(side, h + 1, lane).start()

    @pl.loop(0, heads)
    def _(h):
        at = tile(h, HS)
        for u in range(spans):
            here = pl.ds(u * SPAN, SPAN if u < spans - 1 else TAIL)
            tall = pl.ds(u * reach, reach)
            qu, gu = qall[row, here, at], ogall[row, here, at]
            ku, vu = keys[tall, at], values[tall, at]
            raised = jnp.exp(contract_cols(qu, ku) * scale)
            shares = raised / jnp.sum(raised, axis=-1, keepdims=True)
            share_bf = shares.astype(BF)
            mixed[here, at] = jnp.dot(share_bf, vu, preferred_element_type=F32).astype(BF)
            share_grad = contract_cols(gu, vu)
            centre = jnp.sum(shares * share_grad, axis=-1, keepdims=True)
            score_grad = (shares * (share_grad - centre) * scale).astype(BF)
            qgall[row, here, at] = jnp.dot(
                score_grad, ku, preferred_element_type=F32
            ).astype(BF)
            kg[tall, at] = contract_rows(score_grad, qu).astype(BF)
            vg[tall, at] = contract_rows(share_bf, gu).astype(BF)
            zall[row, h, 0, here, :] = score_grad
            zall[row, h, 1, here, :] = share_bf
        push(h)

    push(heads)

    for k in range(1, seqs):
        came = over(k)
        z_came(ext.at[came, pl.ds(rows, share)], 3, came).wait_recv()

        @pl.when(me < pieces)
        def _():
            z_came(ext.at[came, pl.ds(0, rows)], 2, came).wait_recv()
            token_copy(k).wait_send()

        state_copy(k).wait_send()

    spread(ext, extall, e_send, e_recv)
    mine = pltpu.make_async_copy(ext, extall.at[me], p_sem.at[n])
    mine.start()
    sent(hid, whole, h_send, h_recv)
    sent(nb, every, n_send, n_recv)

    def scatter(ref, into, send, recv, k):
        return remote(ref.at[peer(k)], into.at[me], send.at[k], recv.at[me], "tensor", peer(k))

    @pl.loop(0, wk.shape[0] // TILE)
    def _(i):
        part = contract_cols(kg[...], wk[tile(i), :]) + contract_cols(vg[...], wv[tile(i), :])
        for p in range(blocks):
            terms[p, :, tile(i)] = part[p * R:(p + 1) * R].astype(BF)

    terms[blocks] = jnp.zeros_like(terms[0])

    @pl.loop(0, n)
    def _(k):
        for j in range(held):
            place = blocks
            for i in range(blocks):
                place = jnp.where(slot_at(i) == peer(k) * held + j, i, place)
            every[peer(k), j] = terms[place]

    @pl.loop(1, n)
    def _(k):
        scatter(every, n_in, ns_send, ns_recv, k).start()

    @pl.loop(0, heads)
    def _(lane):
        relay(0, lane)

    relay(0, heads)
    pass_on(extall, e_send, e_recv)

    def hidden_term(index):
        whole[index] = contract_cols(qgall[row], w[tile(index, depth), :]).astype(BF)

    @pl.loop(1, n)
    def _(k):
        hidden_term(peer(k))
        scatter(whole, h_in, hs_send, hs_recv, k).start()

    hidden_term(me)
    rest(extall, e_send, e_recv)
    mine.wait()

    def pick_copy(t):
        return pltpu.make_async_copy(
            extall.at[t, :, pl.ds(rows, share)], states.at[:, tile(t, share)], p_sem.at[t]
        )

    @pl.loop(0, n)
    def _(t):
        pick_copy(t).start()

    @pl.loop(0, n)
    def _(t):
        pick_copy(t).wait()

    for k in range(1, seqs):
        for lane, out in ((0, ogall), (1, qall)):
            z_came(out.at[over(k)], lane, over(k)).wait_recv()

    def add(origin, key_ref, value_ref):
        picks[...] = states[origin].T

        @pl.loop(0, width // TILE)
        def _(i):
            gk[:, tile(i)] += jnp.dot(picks[...], key_ref[:, tile(i)], preferred_element_type=F32)
            gv[:, tile(i)] += jnp.dot(picks[...], value_ref[:, tile(i)], preferred_element_type=F32)

    def rebuild(origin):
        @pl.loop(0, heads)
        def _(h):
            for lane, right, out in ((0, qall, keys), (1, ogall, values)):
                for u in range(spans):
                    here = pl.ds(u * SPAN, SPAN if u < spans - 1 else TAIL)
                    out[pl.ds(u * reach, reach), tile(h, HS)] = contract_rows(
                        zall[origin, h, lane, here, :], right[origin, here, tile(h, HS)]
                    ).astype(BF)

        add(origin, keys, values)

    gk[...] = jnp.zeros_like(gk)
    gv[...] = jnp.zeros_like(gv)
    add(row, kg, vg)
    for h in range(seqs - 1):
        if h > 0:
            @pl.loop(0, heads)
            def _(lane):
                relay(h, lane)

            relay(h, heads)
        for side in range(2):
            @pl.when(arrives(side, h))
            def _():
                rebuild(row - (1 - 2 * side) * (h + 1))

    for ref, into, send, recv, out in (
        (every, n_in, ns_send, ns_recv, nbr), (whole, h_in, hs_send, hs_recv, hid_out)
    ):
        @pl.loop(1, n)
        def _(k):
            remote(
                into.at[peer(k)], into.at[peer(k)], send.at[0], recv.at[peer(k)],
                "tensor", peer(k),
            ).wait_recv()

        into[me] = ref[me]
        total = into[0].astype(F32)
        for j in range(1, n):
            total = total + into[j].astype(F32)
        out[...] = total.astype(BF)

    for side in range(2):
        for h in range(seqs - 1):
            @pl.when(sends(side, h))
            def _():
                @pl.loop(0, heads)
                def _(lane):
                    hop(side, h, lane).wait_send()

                hop(side, h, heads).wait_send()

    sent(ext, extall, e_send, e_recv)
    for k in range(1, seqs):
        z_copy(ogall, 0, k).wait_send()
        z_copy(qall, 1, k).wait_send()

    @pl.loop(1, n)
    def _(k):
        scatter(whole, h_in, hs_send, hs_recv, k).wait_send()
        scatter(every, n_in, ns_send, ns_recv, k).wait_send()


def run(n, seqs, spans, slots, hid, nb, og, w_query, w_key, w_value):
    length, depth = hid.shape
    width = w_query.shape[1]
    heads = width // HS
    rows = (spans - 1) * SPAN + TAIL
    many = slots.shape[0] * slots.shape[1] * R
    cut, reach = DE // seqs, many // spans
    ext = (seqs, rows + many // n, cut)
    dma = pltpu.SemaphoreType.DMA

    def buf(*shape):
        return pltpu.VMEM(shape, BF)

    return pl.pallas_call(
        functools.partial(kernel, n, seqs, spans),
        out_shape=(
            jax.ShapeDtypeStruct((rows, width), BF),
            jax.ShapeDtypeStruct((rows, depth), BF),
            jax.ShapeDtypeStruct(nb.shape, BF),
            jax.ShapeDtypeStruct((seqs, rows, width), BF),
            jax.ShapeDtypeStruct((n,) + ext, BF),
            jax.ShapeDtypeStruct((cut, width), F32),
            jax.ShapeDtypeStruct((cut, width), F32),
        ),
        in_specs=[pl.BlockSpec(memory_space=pltpu.SMEM), VMEM, VMEM, VMEM, ANY, ANY, ANY],
        out_specs=(VMEM, VMEM, VMEM, VMEM, ANY, VMEM, VMEM),
        scratch_shapes=[
            buf(*w_query.shape), buf(*w_key.shape), buf(*w_value.shape),
            pltpu.VMEM((rows, width), F32),
            buf(rows, depth), buf(n, rows, depth), buf(n, *nb.shape), buf(seqs, many, cut),
            buf(many, width), buf(many, width), buf(many, width), buf(many, width),
            buf(seqs, rows, width), buf(seqs, rows, width), buf(*ext),
            buf(n, rows, depth), buf(n, *nb.shape), buf(many // R + 1, R, DE),
            buf(seqs, heads, 2, rows, reach), buf(cut, many),
            dma((3,)), dma((n + 1,)),
            dma((n,)), dma((n,)), dma((n,)), dma((n,)), dma((4, seqs)), dma((4, seqs)),
            dma((n,)), dma((n,)), dma((n,)), dma((n,)), dma((n,)), dma((n,)),
            dma((2, seqs - 1, heads + 1)), dma((2, seqs - 1, heads + 1)),
        ],
        compiler_params=pltpu.CompilerParams(
            collective_id=0, has_side_effects=True, vmem_limit_bytes=LIMIT
        ),
        name="fused",
    )(slots, hid, nb, og, w_query, w_key, w_value)


def body(n, seqs, hidden, neighbours, slot_of, w_query, w_key, w_value, out_grad):
    width = w_query.shape[1]
    length = hidden.shape[1]
    spans = slot_of.shape[1]
    lag = SPAN - 1
    mixed, hid, nbr, qgall, extall, wk, wv = run(
        n, seqs, spans, slot_of[0], hidden[0], neighbours[0], out_grad[0],
        w_query, w_key, w_value,
    )
    rows = mixed.shape[0]

    def back(x):
        return jnp.pad(x[: length - lag], ((lag, 0), (0, 0)))[None]

    pieces = w_query.shape[0] // seqs // extall.shape[3]
    query_part = lax.dot_general(
        extall[:pieces, :, :rows].transpose(0, 3, 1, 2).reshape(-1, seqs * rows),
        qgall.reshape(seqs * rows, width),
        (((1,), (0,)), ((), ())),
        preferred_element_type=F32,
    )
    return (back(mixed), back(hid), nbr[None], query_part, wk, wv)


def solution(mesh):
    return jax.shard_map(
        functools.partial(body, mesh.shape["tensor"], mesh.shape["seq"]),
        mesh=mesh,
        in_specs=(
            P("seq", None, "tensor"),
            P("seq", "tensor", None, None),
            P("seq", None, None),
            P(None, "tensor"),
            P(None, "tensor"),
            P(None, "tensor"),
            P("seq", None, "tensor"),
        ),
        out_specs=(
            P("seq", None, "tensor"),
            P("seq", None, "tensor"),
            P("seq", "tensor", None, None),
            P("seq", "tensor"),
            P("seq", "tensor"),
            P("seq", "tensor"),
        ),
        check_vma=False,
    )
```

```python
import functools
import math

import jax
import jax.numpy as jnp
from jax import lax
from jax.experimental import pallas as pl
from jax.experimental.pallas import tpu as pltpu
from jax.sharding import PartitionSpec as P

HS = 128
DE = 1024
SPAN = 64
R = 128
TAIL = 16
MESH = pl.DeviceIdType.MESH
BF = jnp.bfloat16
F32 = jnp.float32
VMEM = pl.BlockSpec(memory_space=pltpu.VMEM)
ANY = pl.BlockSpec(memory_space=pl.ANY)
LIMIT = 63 * 2**20
TILE = 256


def contract_rows(left, right):
    return lax.dot_general(left, right, (((0,), (0,)), ((), ())), preferred_element_type=F32)


def contract_cols(left, right):
    return lax.dot_general(left, right, (((1,), (1,)), ((), ())), preferred_element_type=F32)


def remote(src, dst, send, recv, axis, index):
    return pltpu.make_async_remote_copy(
        src_ref=src, dst_ref=dst, send_sem=send, recv_sem=recv,
        device_id={axis: index}, device_id_type=MESH,
    )


def kernel(
    n, seqs, spans, slots, hid_in, nb, og_in, w_hbm, wk_hbm, wv_hbm,
    mixed, hid_out, nbr, qgall, extall, gk, gv,
    w, wk, wv, acc, hid, whole, every, states, keys, values, kg, vg, qall, ogall, ext,
    h_in, n_in, terms, zall, zlast, last, picks,
    w_sem, p_sem, h_send, h_recv, n_send, n_recv, z_send, z_recv,
    e_send, e_recv, hs_send, hs_recv, ns_send, ns_recv, line_send, line_recv,
):
    me = lax.axis_index("tensor")
    row = lax.axis_index("seq")
    chips = n // 2
    core = lax.rem(me, 2)
    chip = me // 2
    twin = me + 1 - 2 * core
    rows, depth = hid.shape
    _, many, cut = states.shape
    width = acc.shape[1]
    heads = width // HS
    share, reach = many // n, many // spans
    pieces = n * depth // seqs // cut
    blocks = many // R
    held = every.shape[1]
    near = slots.shape[1]
    scale = 1.0 / math.sqrt(HS)

    def mate(k):
        return lax.rem(chip + k, chips) * 2 + core

    def peer(k):
        return lax.rem(me + k, n)

    def over(k):
        return lax.rem(row + k, seqs)

    def tile(i, size=TILE):
        return pl.ds(pl.multiple_of(i * size, size), size)

    def slot_at(i):
        return slots[i // near, i % near]

    fetches = [
        pltpu.make_async_copy(src, dst, w_sem.at[i])
        for i, (src, dst) in enumerate(((w_hbm, w), (wk_hbm, wk), (wv_hbm, wv)))
    ]
    for fetch in fetches:
        fetch.start()
    barrier = pltpu.get_barrier_semaphore()

    @pl.loop(1, n)
    def _(k):
        pl.semaphore_signal(barrier, inc=1, device_id={"tensor": peer(k)}, device_id_type=MESH)

    for k in range(1, seqs):
        pl.semaphore_signal(barrier, inc=1, device_id={"seq": over(k)}, device_id_type=MESH)

    length = hid_in.shape[0]
    for ref, out in ((hid_in, hid), (og_in, ogall.at[row])):
        whole_rows = ref[pl.ds(length - rows, rows), :].astype(F32)
        moved = pltpu.roll(whole_rows, rows - (SPAN - 1 - (length - rows)), 0)
        at = lax.broadcasted_iota(jnp.int32, moved.shape, 0)
        out[...] = jnp.where(at < length - SPAN + 1, moved, 0.0).astype(BF)
    pl.semaphore_wait(barrier, n - 1 + seqs - 1)

    def own(ref, out, send, recv, k, target):
        return remote(ref, out.at[me], send.at[k], recv.at[me], "tensor", target)

    def onward(out, send, recv, k):
        return remote(
            out.at[mate(k)], out.at[mate(k)], send.at[chips + k], recv.at[mate(k)], "tensor", twin
        )

    def arrival(out, send, recv, index):
        return remote(out.at[index], out.at[index], send.at[0], recv.at[index], "tensor", twin)

    def spread(ref, out, send, recv):
        @pl.loop(1, chips)
        def _(k):
            own(ref, out, send, recv, k, mate(k)).start()

        own(ref, out, send, recv, 0, twin).start()

    def pass_on(out, send, recv, use=None):
        @pl.loop(1, chips)
        def _(k):
            arrival(out, send, recv, mate(k)).wait_recv()
            onward(out, send, recv, k).start()
            if use is not None:
                use(mate(k))

    def rest(out, send, recv, use=None):
        @pl.loop(0, chips)
        def _(k):
            index = mate(k) + 1 - 2 * core
            arrival(out, send, recv, index).wait_recv()
            if use is not None:
                use(index)

    def sent(ref, out, send, recv):
        own(ref, out, send, recv, 0, twin).wait_send()

        @pl.loop(1, chips)
        def _(k):
            own(ref, out, send, recv, k, mate(k)).wait_send()
            onward(out, send, recv, k).wait_send()

    def z_copy(out, lane, k):
        return remote(
            out.at[row], out.at[row], z_send.at[lane, k], z_recv.at[lane, row], "seq", over(k)
        )

    def token_part(dest):
        at = (dest * pieces + me) * cut
        return at // depth, pl.ds(pl.multiple_of(lax.rem(at, depth), cut), cut)

    def state_part(dest):
        return dest, tile(me, share)

    def token_copy(k):
        block, cols = token_part(over(k))
        return remote(
            whole.at[block, :, cols], ext.at[row, pl.ds(0, rows)],
            z_send.at[2, k], z_recv.at[2, row], "seq", over(k),
        )

    def state_copy(k):
        return remote(
            states.at[state_part(over(k))], ext.at[row, pl.ds(rows, share)],
            z_send.at[3, k], z_recv.at[3, row], "seq", over(k),
        )

    def z_came(ref, lane, index):
        return remote(ref, ref, z_send.at[lane, 0], z_recv.at[lane, index], "seq", index)

    spread(hid, whole, h_send, h_recv)
    spread(nb, every, n_send, n_recv)
    for k in range(1, seqs):
        z_copy(ogall, 0, k).start()
    whole[me] = hid[...]
    every[me] = nb[...]
    fetches[0].wait()

    def project(index):
        acc[...] += jnp.dot(whole[index], w[tile(index, depth), :], preferred_element_type=F32)

    acc[...] = jnp.zeros_like(acc)
    project(me)
    pass_on(whole, h_send, h_recv, project)
    rest(whole, h_send, h_recv, project)

    @pl.when(me < pieces)
    def _():
        for k in range(1, seqs):
            token_copy(k).start()
        block, cols = token_part(row)
        ext[row, pl.ds(0, rows), :] = whole[block, :, cols]

    qall[row] = acc[...].astype(BF)
    for k in range(1, seqs):
        z_copy(qall, 1, k).start()
    pass_on(every, n_send, n_recv)
    rest(every, n_send, n_recv)
    for i in range(blocks):
        slot = slot_at(i)
        block = every[slot, 0] if held == 1 else every[slot // held, slot % held]
        for part in range(seqs):
            states[part, pl.ds(i * R, R), :] = block[:, part * cut:(part + 1) * cut]
    for k in range(1, seqs):
        state_copy(k).start()
    ext[row, pl.ds(rows, share), :] = states[row, tile(me, share), :]
    for fetch in fetches[1:]:
        fetch.wait()

    @pl.loop(0, width // TILE)
    def _(i):
        for out, weight in ((keys, wk), (values, wv)):
            total = jnp.zeros((many, TILE), F32)
            for part in range(seqs):
                total += jnp.dot(
                    states[part], weight[pl.ds(part * cut, cut), tile(i)],
                    preferred_element_type=F32,
                )
            out[:, tile(i)] = total.astype(BF)

    def lane_ref(origin, lane):
        if isinstance(lane, int):
            return (zlast if lane == heads else qgall).at[origin]
        return zall.at[origin, lane]

    def hop(side, h, lane):
        step = 1 - 2 * side
        ref = lane_ref(row - step * h, lane)
        return remote(
            ref, ref, line_send.at[side, h, lane], line_recv.at[side, h, lane], "seq", row + step
        )

    def sends(side, h):
        if side == 0:
            return (row - h >= 0) & (row + 1 < seqs)
        return (row + h < seqs) & (row >= 1)

    def arrives(side, h):
        return row - 1 - h >= 0 if side == 0 else row + 1 + h < seqs

    def arrived(side, h, lane):
        step = 1 - 2 * side
        ref = lane_ref(row - step * (h + 1), lane)
        return remote(
            ref, ref, line_send.at[side, h, lane], line_recv.at[side, h, lane], "seq", row - step
        )

    def push(lane):
        for side in range(2):
            @pl.when(sends(side, 0))
            def _():
                hop(side, 0, lane).start()

    def relay(h, lane):
        for side in range(2):
            @pl.when(arrives(side, h))
            def _():
                arrived(side, h, lane).wait_recv()

            if h + 1 < seqs - 1:
                @pl.when(sends(side, h + 1))
                def _():
                    hop(side, h + 1, lane).start()

    token = lax.broadcasted_iota(jnp.int32, last.shape[1:], 0)
    last[...] = jnp.zeros_like(last)

    @pl.loop(0, heads)
    def _(h):
        at = tile(h, HS)
        for u in range(spans):
            here = pl.ds(u * SPAN, SPAN if u < spans - 1 else TAIL)
            tall = pl.ds(u * reach, reach)
            qu, gu = qall[row, here, at], ogall[row, here, at]
            ku, vu = keys[tall, at], values[tall, at]
            raised = jnp.exp(contract_cols(qu, ku) * scale)
            shares = raised / jnp.sum(raised, axis=-1, keepdims=True)
            share_bf = shares.astype(BF)
            mixed[here, at] = jnp.dot(share_bf, vu, preferred_element_type=F32).astype(BF)
            share_grad = contract_cols(gu, vu)
            centre = jnp.sum(shares * share_grad, axis=-1, keepdims=True)
            score_grad = (shares * (share_grad - centre) * scale).astype(BF)
            qgall[row, here, at] = jnp.dot(
                score_grad, ku, preferred_element_type=F32
            ).astype(BF)
            kg[tall, at] = contract_rows(score_grad, qu).astype(BF)
            vg[tall, at] = contract_rows(share_bf, gu).astype(BF)
            for lane, kept in ((0, score_grad), (1, share_bf)):
                if u < spans - 1:
                    zall[row, h, lane, here, :] = kept
                else:
                    last[lane] += jnp.where(token == h, kept.astype(F32)[0:1], 0.0)
        push(h)

    zlast[row] = last[...].astype(BF)
    push(heads)
    push(heads + 1)

    for k in range(1, seqs):
        came = over(k)
        z_came(ext.at[came, pl.ds(rows, share)], 3, came).wait_recv()

        @pl.when(me < pieces)
        def _():
            z_came(ext.at[came, pl.ds(0, rows)], 2, came).wait_recv()
            token_copy(k).wait_send()

        state_copy(k).wait_send()

    spread(ext, extall, e_send, e_recv)
    mine = pltpu.make_async_copy(ext, extall.at[me], p_sem.at[n])
    mine.start()
    sent(hid, whole, h_send, h_recv)
    sent(nb, every, n_send, n_recv)

    def scatter(ref, into, send, recv, k):
        return remote(ref.at[peer(k)], into.at[me], send.at[k], recv.at[me], "tensor", peer(k))

    @pl.loop(0, wk.shape[0] // TILE)
    def _(i):
        part = contract_cols(kg[...], wk[tile(i), :]) + contract_cols(vg[...], wv[tile(i), :])
        for p in range(blocks):
            terms[p, :, tile(i)] = part[p * R:(p + 1) * R].astype(BF)

    terms[blocks] = jnp.zeros_like(terms[0])

    @pl.loop(0, n)
    def _(k):
        for j in range(held):
            place = blocks
            for i in range(blocks):
                place = jnp.where(slot_at(i) == peer(k) * held + j, i, place)
            every[peer(k), j] = terms[place]

    @pl.loop(1, n)
    def _(k):
        scatter(every, n_in, ns_send, ns_recv, k).start()

    @pl.loop(0, heads)
    def _(lane):
        relay(0, lane)

    relay(0, heads)
    relay(0, heads + 1)
    pass_on(extall, e_send, e_recv)

    def hidden_term(index):
        whole[index] = contract_cols(qgall[row], w[tile(index, depth), :]).astype(BF)

    @pl.loop(1, n)
    def _(k):
        hidden_term(peer(k))
        scatter(whole, h_in, hs_send, hs_recv, k).start()

    hidden_term(me)
    rest(extall, e_send, e_recv)
    mine.wait()

    def pick_copy(t):
        return pltpu.make_async_copy(
            extall.at[t, :, pl.ds(rows, share)], states.at[:, tile(t, share)], p_sem.at[t]
        )

    @pl.loop(0, n)
    def _(t):
        pick_copy(t).start()

    @pl.loop(0, n)
    def _(t):
        pick_copy(t).wait()

    for k in range(1, seqs):
        for lane, out in ((0, ogall), (1, qall)):
            z_came(out.at[over(k)], lane, over(k)).wait_recv()

    def add(origin, key_ref, value_ref):
        picks[...] = states[origin].T

        @pl.loop(0, width // TILE)
        def _(i):
            gk[:, tile(i)] += jnp.dot(picks[...], key_ref[:, tile(i)], preferred_element_type=F32)
            gv[:, tile(i)] += jnp.dot(picks[...], value_ref[:, tile(i)], preferred_element_type=F32)

    operands = ((0, qall, keys), (1, ogall, values))

    def rebuild_head(origin, h):
        at = tile(h, HS)
        for lane, right, out in operands:
            for u in range(spans - 1):
                here = pl.ds(u * SPAN, SPAN)
                out[pl.ds(u * reach, reach), at] = contract_rows(
                    zall[origin, h, lane, here, :], right[origin, here, at]
                ).astype(BF)

    def rebuild_last(origin):
        @pl.loop(0, heads)
        def _(h):
            at = tile(h, HS)
            for lane, right, out in operands:
                mine_only = jnp.where(token == h, zlast[origin, lane].astype(F32), 0.0).astype(BF)
                only = right[origin, pl.ds((spans - 1) * SPAN, TAIL), at].astype(F32)
                only = jnp.sum(only, axis=0, keepdims=True)
                only = jnp.broadcast_to(only, (TAIL, HS)).astype(BF)
                out[pl.ds((spans - 1) * reach, reach), at] = contract_rows(
                    mine_only, only
                ).astype(BF)

    gk[...] = jnp.zeros_like(gk)
    gv[...] = jnp.zeros_like(gv)
    add(row, kg, vg)
    for h in range(seqs - 1):
        final = h == seqs - 2
        origins = [row - (1 - 2 * side) * (h + 1) for side in range(2)]
        if h > 0:
            @pl.loop(0, heads)
            def _(lane):
                relay(h, lane)
                if final:
                    for side in range(2):
                        @pl.when(arrives(side, h))
                        def _():
                            rebuild_head(origins[side], lane)

            relay(h, heads)
            if not final:
                relay(h, heads + 1)
        for side in range(2):
            @pl.when(arrives(side, h))
            def _():
                if not (final and h > 0):
                    @pl.loop(0, heads)
                    def _(lane):
                        rebuild_head(origins[side], lane)

                rebuild_last(origins[side])
                add(origins[side], keys, values)

        if final and h > 0:
            relay(h, heads + 1)

    for ref, into, send, recv, out in (
        (every, n_in, ns_send, ns_recv, nbr), (whole, h_in, hs_send, hs_recv, hid_out)
    ):
        @pl.loop(1, n)
        def _(k):
            remote(
                into.at[peer(k)], into.at[peer(k)], send.at[0], recv.at[peer(k)],
                "tensor", peer(k),
            ).wait_recv()

        into[me] = ref[me]
        total = into[0].astype(F32)
        for j in range(1, n):
            total = total + into[j].astype(F32)
        out[...] = total.astype(BF)

    for side in range(2):
        for h in range(seqs - 1):
            @pl.when(sends(side, h))
            def _():
                @pl.loop(0, heads)
                def _(lane):
                    hop(side, h, lane).wait_send()

                hop(side, h, heads).wait_send()
                hop(side, h, heads + 1).wait_send()

    sent(ext, extall, e_send, e_recv)
    for k in range(1, seqs):
        z_copy(ogall, 0, k).wait_send()
        z_copy(qall, 1, k).wait_send()

    @pl.loop(1, n)
    def _(k):
        scatter(whole, h_in, hs_send, hs_recv, k).wait_send()
        scatter(every, n_in, ns_send, ns_recv, k).wait_send()


def run(n, seqs, spans, slots, hid, nb, og, w_query, w_key, w_value):
    length, depth = hid.shape
    width = w_query.shape[1]
    heads = width // HS
    rows = (spans - 1) * SPAN + TAIL
    many = slots.shape[0] * slots.shape[1] * R
    cut, reach = DE // seqs, many // spans
    ext = (seqs, rows + many // n, cut)
    dma = pltpu.SemaphoreType.DMA

    def buf(*shape):
        return pltpu.VMEM(shape, BF)

    return pl.pallas_call(
        functools.partial(kernel, n, seqs, spans),
        out_shape=(
            jax.ShapeDtypeStruct((rows, width), BF),
            jax.ShapeDtypeStruct((rows, depth), BF),
            jax.ShapeDtypeStruct(nb.shape, BF),
            jax.ShapeDtypeStruct((seqs, rows, width), BF),
            jax.ShapeDtypeStruct((n,) + ext, BF),
            jax.ShapeDtypeStruct((cut, width), F32),
            jax.ShapeDtypeStruct((cut, width), F32),
        ),
        in_specs=[pl.BlockSpec(memory_space=pltpu.SMEM), VMEM, VMEM, VMEM, ANY, ANY, ANY],
        out_specs=(VMEM, VMEM, VMEM, VMEM, ANY, VMEM, VMEM),
        scratch_shapes=[
            buf(*w_query.shape), buf(*w_key.shape), buf(*w_value.shape),
            pltpu.VMEM((rows, width), F32),
            buf(rows, depth), buf(n, rows, depth), buf(n, *nb.shape), buf(seqs, many, cut),
            buf(many, width), buf(many, width), buf(many, width), buf(many, width),
            buf(seqs, rows, width), buf(seqs, rows, width), buf(*ext),
            buf(n, rows, depth), buf(n, *nb.shape), buf(many // R + 1, R, DE),
            buf(seqs, heads, 2, rows - TAIL, reach), buf(seqs, 2, TAIL, reach),
            pltpu.VMEM((2, TAIL, reach), F32), buf(cut, many),
            dma((3,)), dma((n + 1,)),
            dma((n,)), dma((n,)), dma((n,)), dma((n,)), dma((4, seqs)), dma((4, seqs)),
            dma((n,)), dma((n,)), dma((n,)), dma((n,)), dma((n,)), dma((n,)),
            dma((2, seqs - 1, heads + 2)), dma((2, seqs - 1, heads + 2)),
        ],
        compiler_params=pltpu.CompilerParams(
            collective_id=0, has_side_effects=True, vmem_limit_bytes=LIMIT
        ),
        name="fused",
    )(slots, hid, nb, og, w_query, w_key, w_value)


def body(n, seqs, hidden, neighbours, slot_of, w_query, w_key, w_value, out_grad):
    width = w_query.shape[1]
    length = hidden.shape[1]
    spans = slot_of.shape[1]
    lag = SPAN - 1
    mixed, hid, nbr, qgall, extall, wk, wv = run(
        n, seqs, spans, slot_of[0], hidden[0], neighbours[0], out_grad[0],
        w_query, w_key, w_value,
    )
    rows = mixed.shape[0]

    def back(x):
        return jnp.pad(x[: length - lag], ((lag, 0), (0, 0)))[None]

    pieces = w_query.shape[0] // seqs // extall.shape[3]
    query_part = lax.dot_general(
        extall[:pieces, :, :rows].transpose(0, 3, 1, 2).reshape(-1, seqs * rows),
        qgall.reshape(seqs * rows, width),
        (((1,), (0,)), ((), ())),
        preferred_element_type=F32,
    )
    return (back(mixed), back(hid), nbr[None], query_part, wk, wv)


def solution(mesh):
    return jax.shard_map(
        functools.partial(body, mesh.shape["tensor"], mesh.shape["seq"]),
        mesh=mesh,
        in_specs=(
            P("seq", None, "tensor"),
            P("seq", "tensor", None, None),
            P("seq", None, None),
            P(None, "tensor"),
            P(None, "tensor"),
            P(None, "tensor"),
            P("seq", None, "tensor"),
        ),
        out_specs=(
            P("seq", None, "tensor"),
            P("seq", None, "tensor"),
            P("seq", "tensor", None, None),
            P("seq", "tensor"),
            P("seq", "tensor"),
            P("seq", "tensor"),
        ),
        check_vma=False,
    )
```

```python
import functools
import math

import jax
import jax.numpy as jnp
from jax import lax
from jax.experimental import pallas as pl
from jax.experimental.pallas import tpu as pltpu
from jax.sharding import PartitionSpec as P

HS = 128
DE = 1024
SPAN = 64
R = 128
TAIL = 16
MESH = pl.DeviceIdType.MESH
BF = jnp.bfloat16
F32 = jnp.float32
VMEM = pl.BlockSpec(memory_space=pltpu.VMEM)
ANY = pl.BlockSpec(memory_space=pl.ANY)
LIMIT = 63 * 2**20
TILE = 256


def contract_rows(left, right):
    return lax.dot_general(left, right, (((0,), (0,)), ((), ())), preferred_element_type=F32)


def contract_cols(left, right):
    return lax.dot_general(left, right, (((1,), (1,)), ((), ())), preferred_element_type=F32)


def remote(src, dst, send, recv, axis, index):
    return pltpu.make_async_remote_copy(
        src_ref=src, dst_ref=dst, send_sem=send, recv_sem=recv,
        device_id={axis: index}, device_id_type=MESH,
    )


def kernel(
    n, seqs, spans, slots, hid_in, nb, og_in, w_hbm, wk_hbm, wv_hbm,
    mixed, hid_out, nbr, qgall, extall, gk, gv,
    w, wk, wv, acc, hid, whole, every, states, keys, values, kg, vg, qall, ogall, ext,
    h_in, n_in, terms, zall, zlast, last, picks,
    w_sem, p_sem, h_send, h_recv, n_send, n_recv, z_send, z_recv,
    e_send, e_recv, hs_send, hs_recv, ns_send, ns_recv, line_send, line_recv,
):
    me = lax.axis_index("tensor")
    row = lax.axis_index("seq")
    chips = n // 2
    core = lax.rem(me, 2)
    chip = me // 2
    twin = me + 1 - 2 * core
    rows, depth = hid.shape
    _, many, cut = states.shape
    width = acc.shape[1]
    heads = width // HS
    share, reach = many // n, many // spans
    pieces = n * depth // seqs // cut
    blocks = many // R
    held = every.shape[1]
    near = slots.shape[1]
    scale = 1.0 / math.sqrt(HS)

    def mate(k):
        return lax.rem(chip + k, chips) * 2 + core

    def peer(k):
        return lax.rem(me + k, n)

    def over(k):
        return lax.rem(row + k, seqs)

    def tile(i, size=TILE):
        return pl.ds(pl.multiple_of(i * size, size), size)

    def slot_at(i):
        return slots[i // near, i % near]

    fetches = [
        pltpu.make_async_copy(src, dst, w_sem.at[i])
        for i, (src, dst) in enumerate(((w_hbm, w), (wk_hbm, wk), (wv_hbm, wv)))
    ]
    for fetch in fetches:
        fetch.start()
    barrier = pltpu.get_barrier_semaphore()

    @pl.loop(1, n)
    def _(k):
        pl.semaphore_signal(barrier, inc=1, device_id={"tensor": peer(k)}, device_id_type=MESH)

    for k in range(1, seqs):
        pl.semaphore_signal(barrier, inc=1, device_id={"seq": over(k)}, device_id_type=MESH)

    length = hid_in.shape[0]
    for ref, out in ((hid_in, hid), (og_in, ogall.at[row])):
        whole_rows = ref[pl.ds(length - rows, rows), :].astype(F32)
        moved = pltpu.roll(whole_rows, rows - (SPAN - 1 - (length - rows)), 0)
        at = lax.broadcasted_iota(jnp.int32, moved.shape, 0)
        out[...] = jnp.where(at < length - SPAN + 1, moved, 0.0).astype(BF)
    pl.semaphore_wait(barrier, n - 1 + seqs - 1)

    def own(ref, out, send, recv, k, target):
        return remote(ref, out.at[me], send.at[k], recv.at[me], "tensor", target)

    def onward(out, send, recv, k):
        return remote(
            out.at[mate(k)], out.at[mate(k)], send.at[chips + k], recv.at[mate(k)], "tensor", twin
        )

    def arrival(out, send, recv, index):
        return remote(out.at[index], out.at[index], send.at[0], recv.at[index], "tensor", twin)

    def spread(ref, out, send, recv):
        @pl.loop(1, chips)
        def _(k):
            own(ref, out, send, recv, k, mate(k)).start()

        own(ref, out, send, recv, 0, twin).start()

    def pass_on(out, send, recv, use=None):
        @pl.loop(1, chips)
        def _(k):
            arrival(out, send, recv, mate(k)).wait_recv()
            onward(out, send, recv, k).start()
            if use is not None:
                use(mate(k))

    def rest(out, send, recv, use=None):
        @pl.loop(0, chips)
        def _(k):
            index = mate(k) + 1 - 2 * core
            arrival(out, send, recv, index).wait_recv()
            if use is not None:
                use(index)

    def sent(ref, out, send, recv):
        own(ref, out, send, recv, 0, twin).wait_send()

        @pl.loop(1, chips)
        def _(k):
            own(ref, out, send, recv, k, mate(k)).wait_send()
            onward(out, send, recv, k).wait_send()

    def z_copy(out, lane, k):
        return remote(
            out.at[row], out.at[row], z_send.at[lane, k], z_recv.at[lane, row], "seq", over(k)
        )

    def token_part(dest):
        at = (dest * pieces + me) * cut
        return at // depth, pl.ds(pl.multiple_of(lax.rem(at, depth), cut), cut)

    def state_part(dest):
        return dest, tile(me, share)

    def token_copy(k):
        block, cols = token_part(over(k))
        return remote(
            whole.at[block, :, cols], ext.at[row, pl.ds(0, rows)],
            z_send.at[2, k], z_recv.at[2, row], "seq", over(k),
        )

    def state_copy(k):
        return remote(
            states.at[state_part(over(k))], ext.at[row, pl.ds(rows, share)],
            z_send.at[3, k], z_recv.at[3, row], "seq", over(k),
        )

    def z_came(ref, lane, index):
        return remote(ref, ref, z_send.at[lane, 0], z_recv.at[lane, index], "seq", index)

    spread(hid, whole, h_send, h_recv)
    spread(nb, every, n_send, n_recv)
    for k in range(1, seqs):
        z_copy(ogall, 0, k).start()
    whole[me] = hid[...]
    every[me] = nb[...]
    fetches[0].wait()

    def project(index):
        acc[...] += jnp.dot(whole[index], w[tile(index, depth), :], preferred_element_type=F32)

    acc[...] = jnp.zeros_like(acc)
    project(me)
    pass_on(whole, h_send, h_recv, project)
    rest(whole, h_send, h_recv, project)

    @pl.when(me < pieces)
    def _():
        for k in range(1, seqs):
            token_copy(k).start()
        block, cols = token_part(row)
        ext[row, pl.ds(0, rows), :] = whole[block, :, cols]

    qall[row] = acc[...].astype(BF)
    for k in range(1, seqs):
        z_copy(qall, 1, k).start()
    pass_on(every, n_send, n_recv)
    rest(every, n_send, n_recv)
    for i in range(blocks):
        slot = slot_at(i)
        block = every[slot, 0] if held == 1 else every[slot // held, slot % held]
        for part in range(seqs):
            states[part, pl.ds(i * R, R), :] = block[:, part * cut:(part + 1) * cut]
    for k in range(1, seqs):
        state_copy(k).start()
    ext[row, pl.ds(rows, share), :] = states[row, tile(me, share), :]
    for fetch in fetches[1:]:
        fetch.wait()

    @pl.loop(0, width // TILE)
    def _(i):
        for out, weight in ((keys, wk), (values, wv)):
            total = jnp.zeros((many, TILE), F32)
            for part in range(seqs):
                total += jnp.dot(
                    states[part], weight[pl.ds(part * cut, cut), tile(i)],
                    preferred_element_type=F32,
                )
            out[:, tile(i)] = total.astype(BF)

    def lane_ref(origin, lane):
        if isinstance(lane, int):
            return (zlast if lane == heads else qgall).at[origin]
        return zall.at[origin, lane]

    def hop(side, h, lane):
        step = 1 - 2 * side
        ref = lane_ref(row - step * h, lane)
        return remote(
            ref, ref, line_send.at[side, h, lane], line_recv.at[side, h, lane], "seq", row + step
        )

    def sends(side, h):
        if side == 0:
            return (row - h >= 0) & (row + 1 < seqs)
        return (row + h < seqs) & (row >= 1)

    def arrives(side, h):
        return row - 1 - h >= 0 if side == 0 else row + 1 + h < seqs

    def arrived(side, h, lane):
        step = 1 - 2 * side
        ref = lane_ref(row - step * (h + 1), lane)
        return remote(
            ref, ref, line_send.at[side, h, lane], line_recv.at[side, h, lane], "seq", row - step
        )

    def push(lane):
        for side in range(2):
            @pl.when(sends(side, 0))
            def _():
                hop(side, 0, lane).start()

    def relay(h, lane):
        for side in range(2):
            @pl.when(arrives(side, h))
            def _():
                arrived(side, h, lane).wait_recv()

            if h + 1 < seqs - 1:
                @pl.when(sends(side, h + 1))
                def _():
                    hop(side, h + 1, lane).start()

    token = lax.broadcasted_iota(jnp.int32, last.shape[1:], 0)
    last[...] = jnp.zeros_like(last)

    @pl.loop(0, heads)
    def _(h):
        at = tile(h, HS)
        for u in range(spans):
            here = pl.ds(u * SPAN, SPAN if u < spans - 1 else TAIL)
            tall = pl.ds(u * reach, reach)
            qu, gu = qall[row, here, at], ogall[row, here, at]
            ku, vu = keys[tall, at], values[tall, at]
            raised = jnp.exp(contract_cols(qu, ku) * scale)
            shares = raised / jnp.sum(raised, axis=-1, keepdims=True)
            share_bf = shares.astype(BF)
            mixed[here, at] = jnp.dot(share_bf, vu, preferred_element_type=F32).astype(BF)
            share_grad = contract_cols(gu, vu)
            centre = jnp.sum(shares * share_grad, axis=-1, keepdims=True)
            score_grad = (shares * (share_grad - centre) * scale).astype(BF)
            qgall[row, here, at] = jnp.dot(
                score_grad, ku, preferred_element_type=F32
            ).astype(BF)
            kg[tall, at] = contract_rows(score_grad, qu).astype(BF)
            vg[tall, at] = contract_rows(share_bf, gu).astype(BF)
            for lane, kept in ((0, score_grad), (1, share_bf)):
                if u < spans - 1:
                    zall[row, h, lane, here, :] = kept
                else:
                    last[lane] += jnp.where(token == h, kept.astype(F32)[0:1], 0.0)
        push(h)

    zlast[row] = last[...].astype(BF)
    push(heads)
    push(heads + 1)

    for k in range(1, seqs):
        came = over(k)
        z_came(ext.at[came, pl.ds(rows, share)], 3, came).wait_recv()

        @pl.when(me < pieces)
        def _():
            z_came(ext.at[came, pl.ds(0, rows)], 2, came).wait_recv()
            token_copy(k).wait_send()

        state_copy(k).wait_send()

    spread(ext, extall, e_send, e_recv)
    mine = pltpu.make_async_copy(ext, extall.at[me], p_sem.at[n])
    mine.start()
    sent(hid, whole, h_send, h_recv)
    sent(nb, every, n_send, n_recv)

    def scatter(ref, into, send, recv, k):
        return remote(ref.at[peer(k)], into.at[me], send.at[k], recv.at[me], "tensor", peer(k))

    @pl.loop(0, wk.shape[0] // TILE)
    def _(i):
        part = contract_cols(kg[...], wk[tile(i), :]) + contract_cols(vg[...], wv[tile(i), :])
        for p in range(blocks):
            terms[p, :, tile(i)] = part[p * R:(p + 1) * R].astype(BF)

    terms[blocks] = jnp.zeros_like(terms[0])

    @pl.loop(0, n)
    def _(k):
        for j in range(held):
            place = blocks
            for i in range(blocks):
                place = jnp.where(slot_at(i) == peer(k) * held + j, i, place)
            every[peer(k), j] = terms[place]

    @pl.loop(1, n)
    def _(k):
        scatter(every, n_in, ns_send, ns_recv, k).start()

    @pl.loop(0, heads)
    def _(lane):
        relay(0, lane)

    relay(0, heads)
    relay(0, heads + 1)
    pass_on(extall, e_send, e_recv)

    def hidden_term(index):
        whole[index] = contract_cols(qgall[row], w[tile(index, depth), :]).astype(BF)

    @pl.loop(1, n)
    def _(k):
        hidden_term(peer(k))
        scatter(whole, h_in, hs_send, hs_recv, k).start()

    hidden_term(me)
    rest(extall, e_send, e_recv)
    mine.wait()

    def pick_copy(t):
        return pltpu.make_async_copy(
            extall.at[t, :, pl.ds(rows, share)], states.at[:, tile(t, share)], p_sem.at[t]
        )

    @pl.loop(0, n)
    def _(t):
        pick_copy(t).start()

    @pl.loop(0, n)
    def _(t):
        pick_copy(t).wait()

    for k in range(1, seqs):
        for lane, out in ((0, ogall), (1, qall)):
            z_came(out.at[over(k)], lane, over(k)).wait_recv()

    def add(origin, key_ref, value_ref):
        picks[...] = states[origin].T

        @pl.loop(0, width // TILE)
        def _(i):
            gk[:, tile(i)] += jnp.dot(picks[...], key_ref[:, tile(i)], preferred_element_type=F32)
            gv[:, tile(i)] += jnp.dot(picks[...], value_ref[:, tile(i)], preferred_element_type=F32)

    operands = ((0, qall, keys), (1, ogall, values))

    def rebuild_head(origin, h):
        at = tile(h, HS)
        for lane, right, out in operands:
            for u in range(spans - 1):
                here = pl.ds(u * SPAN, SPAN)
                out[pl.ds(u * reach, reach), at] = contract_rows(
                    zall[origin, h, lane, here, :], right[origin, here, at]
                ).astype(BF)

    def rebuild_last(origin):
        @pl.loop(0, heads)
        def _(h):
            at = tile(h, HS)
            for lane, right, out in operands:
                mine_only = jnp.where(token == h, zlast[origin, lane].astype(F32), 0.0).astype(BF)
                only = right[origin, pl.ds((spans - 1) * SPAN, TAIL), at].astype(F32)
                only = jnp.sum(only, axis=0, keepdims=True)
                only = jnp.broadcast_to(only, (TAIL, HS)).astype(BF)
                out[pl.ds((spans - 1) * reach, reach), at] = contract_rows(
                    mine_only, only
                ).astype(BF)

    gk[...] = jnp.zeros_like(gk)
    gv[...] = jnp.zeros_like(gv)
    add(row, kg, vg)
    for h in range(seqs - 1):
        final = h == seqs - 2
        origins = [row - (1 - 2 * side) * (h + 1) for side in range(2)]
        if final and h > 0:
            @pl.loop(0, heads)
            def _(lane):
                relay(h, lane)
                for side in range(2):
                    @pl.when(arrives(side, h))
                    def _():
                        rebuild_head(origins[side], lane)

            relay(h, heads)
        for side in range(2):
            @pl.when(arrives(side, h))
            def _():
                if not (final and h > 0):
                    @pl.loop(0, heads)
                    def _(lane):
                        rebuild_head(origins[side], lane)

                rebuild_last(origins[side])
                add(origins[side], keys, values)

            if side == 0 and h + 1 < seqs - 2:
                @pl.loop(0, heads)
                def _(lane):
                    relay(h + 1, lane)

                relay(h + 1, heads)
                relay(h + 1, heads + 1)

        if final and h > 0:
            relay(h, heads + 1)

    for ref, into, send, recv, out in (
        (every, n_in, ns_send, ns_recv, nbr), (whole, h_in, hs_send, hs_recv, hid_out)
    ):
        @pl.loop(1, n)
        def _(k):
            remote(
                into.at[peer(k)], into.at[peer(k)], send.at[0], recv.at[peer(k)],
                "tensor", peer(k),
            ).wait_recv()

        into[me] = ref[me]
        total = into[0].astype(F32)
        for j in range(1, n):
            total = total + into[j].astype(F32)
        out[...] = total.astype(BF)

    for side in range(2):
        for h in range(seqs - 1):
            @pl.when(sends(side, h))
            def _():
                @pl.loop(0, heads)
                def _(lane):
                    hop(side, h, lane).wait_send()

                hop(side, h, heads).wait_send()
                hop(side, h, heads + 1).wait_send()

    sent(ext, extall, e_send, e_recv)
    for k in range(1, seqs):
        z_copy(ogall, 0, k).wait_send()
        z_copy(qall, 1, k).wait_send()

    @pl.loop(1, n)
    def _(k):
        scatter(whole, h_in, hs_send, hs_recv, k).wait_send()
        scatter(every, n_in, ns_send, ns_recv, k).wait_send()


def run(n, seqs, spans, slots, hid, nb, og, w_query, w_key, w_value):
    length, depth = hid.shape
    width = w_query.shape[1]
    heads = width // HS
    rows = (spans - 1) * SPAN + TAIL
    many = slots.shape[0] * slots.shape[1] * R
    cut, reach = DE // seqs, many // spans
    ext = (seqs, rows + many // n, cut)
    dma = pltpu.SemaphoreType.DMA

    def buf(*shape):
        return pltpu.VMEM(shape, BF)

    return pl.pallas_call(
        functools.partial(kernel, n, seqs, spans),
        out_shape=(
            jax.ShapeDtypeStruct((rows, width), BF),
            jax.ShapeDtypeStruct((rows, depth), BF),
            jax.ShapeDtypeStruct(nb.shape, BF),
            jax.ShapeDtypeStruct((seqs, rows, width), BF),
            jax.ShapeDtypeStruct((n,) + ext, BF),
            jax.ShapeDtypeStruct((cut, width), F32),
            jax.ShapeDtypeStruct((cut, width), F32),
        ),
        in_specs=[pl.BlockSpec(memory_space=pltpu.SMEM), VMEM, VMEM, VMEM, ANY, ANY, ANY],
        out_specs=(VMEM, VMEM, VMEM, VMEM, ANY, VMEM, VMEM),
        scratch_shapes=[
            buf(*w_query.shape), buf(*w_key.shape), buf(*w_value.shape),
            pltpu.VMEM((rows, width), F32),
            buf(rows, depth), buf(n, rows, depth), buf(n, *nb.shape), buf(seqs, many, cut),
            buf(many, width), buf(many, width), buf(many, width), buf(many, width),
            buf(seqs, rows, width), buf(seqs, rows, width), buf(*ext),
            buf(n, rows, depth), buf(n, *nb.shape), buf(many // R + 1, R, DE),
            buf(seqs, heads, 2, rows - TAIL, reach), buf(seqs, 2, TAIL, reach),
            pltpu.VMEM((2, TAIL, reach), F32), buf(cut, many),
            dma((3,)), dma((n + 1,)),
            dma((n,)), dma((n,)), dma((n,)), dma((n,)), dma((4, seqs)), dma((4, seqs)),
            dma((n,)), dma((n,)), dma((n,)), dma((n,)), dma((n,)), dma((n,)),
            dma((2, seqs - 1, heads + 2)), dma((2, seqs - 1, heads + 2)),
        ],
        compiler_params=pltpu.CompilerParams(
            collective_id=0, has_side_effects=True, vmem_limit_bytes=LIMIT
        ),
        name="fused",
    )(slots, hid, nb, og, w_query, w_key, w_value)


def body(n, seqs, hidden, neighbours, slot_of, w_query, w_key, w_value, out_grad):
    width = w_query.shape[1]
    length = hidden.shape[1]
    spans = slot_of.shape[1]
    lag = SPAN - 1
    mixed, hid, nbr, qgall, extall, wk, wv = run(
        n, seqs, spans, slot_of[0], hidden[0], neighbours[0], out_grad[0],
        w_query, w_key, w_value,
    )
    rows = mixed.shape[0]

    def back(x):
        return jnp.pad(x[: length - lag], ((lag, 0), (0, 0)))[None]

    pieces = w_query.shape[0] // seqs // extall.shape[3]
    query_part = lax.dot_general(
        extall[:pieces, :, :rows].transpose(0, 3, 1, 2).reshape(-1, seqs * rows),
        qgall.reshape(seqs * rows, width),
        (((1,), (0,)), ((), ())),
        preferred_element_type=F32,
    )
    return (back(mixed), back(hid), nbr[None], query_part, wk, wv)


def solution(mesh):
    return jax.shard_map(
        functools.partial(body, mesh.shape["tensor"], mesh.shape["seq"]),
        mesh=mesh,
        in_specs=(
            P("seq", None, "tensor"),
            P("seq", "tensor", None, None),
            P("seq", None, None),
            P(None, "tensor"),
            P(None, "tensor"),
            P(None, "tensor"),
            P("seq", None, "tensor"),
        ),
        out_specs=(
            P("seq", None, "tensor"),
            P("seq", None, "tensor"),
            P("seq", "tensor", None, None),
            P("seq", "tensor"),
            P("seq", "tensor"),
            P("seq", "tensor"),
        ),
        check_vma=False,
    )
```
